256 devices in a mesh: ctx: 32 (over z, x), head: 8 (over y, core).
Axes of the slice: x: 4, y: 4, z: 8, core: 2. Of those that a mesh axis runs over, the one named last changes fastest.
Arguments:
- queries: bfloat16 [16384, 5120], P(('ctx', 'head')), may hold values from -6 to 6
- keys: bfloat16 [16384, 5120], P(('ctx', 'head')), may hold values from -6 to 6
- values: bfloat16 [16384, 5120], P(('ctx', 'head')), may hold values from -6 to 6
- outputs: bfloat16 [16384, 5120], P(('ctx', 'head')), may hold values from -2.5 to 2.5
- out_grad: bfloat16 [16384, 5120], P(('ctx', 'head')), may hold values from -6 to 6
- log_norms: float32 [16384, 40], P('ctx', 'head'), may hold values from 4 to 8
- doc_lengths: int32 [16], replicated, may hold values from 1 to 2048, 16384 in all
Outputs:
- grad_queries: bfloat16 [16384, 5120], P(('ctx', 'head'))
- grad_keys: bfloat16 [16384, 5120], P(('ctx', 'head'))
- grad_values: bfloat16 [16384, 5120], P(('ctx', 'head'))
The draws below stay inside these ranges and needn't reach their ends.
Inputs may be any that keep to these rules, and one draw needn't show every extreme that they name: `doc_lengths`: positive lengths that sum to 16384; the longest document has exactly 2048 tokens.
All inputs are finite; a program needn't handle non-finite values.
Results may differ from the reference program's by a relative error of at most 0.0056.
Values may be sent and summed in bfloat16 or wider, within the bound.
A program may use at most 128 MiB of HBM per device.

```python
import math
import jax
import jax.numpy as jnp
import numpy as np
from jax import lax

HEADS = 40
HD = 128
S_DEV = 512
REACH = 4
TOKENS = 16384
DOCMAX = 2048
NDOCS = 16
N_CTX = 32


def levels(key, shape, split, low, high):
    loudness, own = 1.0, jax.random.fold_in(key, 6)
    for axis_at, parts in split:
        heights = jnp.exp(jax.random.uniform(jax.random.fold_in(own, axis_at), (parts,), jnp.float32, low / len(split), high / len(split)))
        loudness = loudness * jnp.repeat(heights, shape[axis_at] // parts).reshape([-1 if axis == axis_at else 1 for axis in range(len(shape))])
    return loudness


def length_profile(amount, total, reach, slope):
    loads = [(1 << 20) // math.isqrt(rank ** slope) + 1 for rank in range(2, amount + 1)]
    surplus, counts = total - reach - (amount - 1), [1] * (amount - 1)
    while surplus > 0:
        free = [i for i in range(amount - 1) if counts[i] < reach]
        whole, left = sum([loads[i] for i in free]), surplus
        for i in free:
            more = min(reach - counts[i], max(1, left * loads[i] // whole), surplus)
            counts[i] = counts[i] + more
            surplus = surplus - more
    return np.array([reach] + counts)


def uneven_parts(rng, count, total, reach, skew):
    if count == 2:
        one = jax.random.randint(rng, (), max(1, total - reach), min(reach, total - 1) + 1)
        return jnp.stack([one, total - one])
    lengths = jnp.asarray(length_profile(count, total, reach, skew), jnp.int32)
    couples = (count - 1) // 2
    source_of, sink = lengths[1:1 + 2 * couples:2], lengths[2:2 + 2 * couples:2]
    slack = jnp.minimum(source_of - 1, reach - sink)
    passed = jax.random.randint(jax.random.fold_in(rng, 1), (couples,), 0, 1 << 20) % (slack + 1)
    lengths = lengths.at[1:1 + 2 * couples:2].set(source_of - passed).at[2:2 + 2 * couples:2].set(sink + passed)
    return lengths[jax.random.permutation(jax.random.fold_in(rng, 2), count)]


def gaussian(own_key, shape, deviation, bound, pieces=(), kind=jnp.bfloat16):
    values = deviation * jax.random.normal(own_key, shape, jnp.float32)
    if pieces:
        values = values * levels(own_key, shape, pieces, -0.22, 0.18)
    return jnp.clip(values, -bound, bound).astype(kind)


def setup_inputs(seed: int = 0) -> dict:
    key_of = jax.random.split(jax.random.key(seed), 8)
    return {
        "queries": gaussian(key_of[0], (TOKENS, HEADS * HD), 1.0, 6.0, ((0, 256),)),
        "keys": gaussian(key_of[1], (TOKENS, HEADS * HD), 1.0, 6.0, ((0, 256),)),
        "values": gaussian(key_of[2], (TOKENS, HEADS * HD), 1.0, 6.0, ((0, 256),)),
        "outputs": gaussian(key_of[3], (TOKENS, HEADS * HD), 0.3, 2.5, ((0, 256),)),
        "out_grad": gaussian(key_of[4], (TOKENS, HEADS * HD), 1.0, 6.0, ((0, 256),)),
        "log_norms": jnp.clip(4.0 + 4.0 * jax.random.uniform(key_of[5], (TOKENS, HEADS), jnp.float32) ** levels(key_of[5], (TOKENS, HEADS), ((0, 32), (1, 8)), -0.2, 0.2), 4.0, 8.0),
        "doc_lengths": uneven_parts(key_of[6], NDOCS, TOKENS, DOCMAX, 1).astype(jnp.int32),
    }


def doc_number(doc_ends, positions):
    return lax.optimization_barrier(jnp.sum((positions[:, None] >= doc_ends[None, :]).astype(jnp.int32), axis=1)).astype(jnp.int32)

def alive_mask(doc_ends, query_pos, key_pos):
    same_doc = doc_number(doc_ends, query_pos)[:, None] == doc_number(doc_ends, key_pos)[None, :]
    causal = key_pos[None, :] <= query_pos[:, None]
    inside = (key_pos[None, :] >= 0) & (query_pos[:, None] < TOKENS)
    return same_doc & causal & inside

def rounded(array):
    low = array.astype(jnp.bfloat16)
    low = lax.optimization_barrier(low)
    return low.astype(jnp.float32)

def tile_terms(query_rows, key_rows, value_rows, grad_rows, norm_rows, delta_rows, alive):
    scaling = 1.0 / math.sqrt(HD)
    query_f = query_rows.astype(jnp.float32)
    key_f = key_rows.astype(jnp.float32)
    value_f = value_rows.astype(jnp.float32)
    grad_f = grad_rows.astype(jnp.float32)
    scores = jnp.einsum('rhe,che->hrc', query_f, key_f) * scaling
    weights = jnp.where(alive[None], jnp.exp(scores - jnp.transpose(norm_rows)[:, :, None]), 0.0)
    dweights = jnp.einsum('rhe,che->hrc', grad_f, value_f)
    dscore = rounded(weights * (dweights - jnp.transpose(delta_rows)[:, :, None]))
    weights_low = rounded(weights)
    grad_query = jnp.einsum('hrc,che->rhe', dscore, key_f) * scaling
    grad_key = jnp.einsum('hrc,rhe->che', dscore, query_f) * scaling
    grad_value = jnp.einsum('hrc,rhe->che', weights_low, grad_f)
    return (grad_query, grad_key, grad_value)

def reference(queries, keys, values, outputs, out_grad, log_norms, doc_lengths):
    query_all = queries.reshape(TOKENS, HEADS, HD)
    key_all = keys.reshape(TOKENS, HEADS, HD)
    value_all = values.reshape(TOKENS, HEADS, HD)
    output_all = outputs.reshape(TOKENS, HEADS, HD)
    grad_all = out_grad.reshape(TOKENS, HEADS, HD)
    delta = lax.optimization_barrier(jnp.sum(grad_all.astype(jnp.float32) * output_all.astype(jnp.float32), axis=-1))
    doc_ends = jnp.cumsum(doc_lengths).astype(jnp.int32)
    span = REACH * S_DEV
    width = span + S_DEV

    def front(array):
        return jnp.concatenate([jnp.zeros((span,) + array.shape[1:], array.dtype), array], axis=0)

    def back(array):
        return jnp.concatenate([array, jnp.zeros((span,) + array.shape[1:], array.dtype)], axis=0)
    key_front = front(key_all)
    value_front = front(value_all)
    query_back = back(query_all)
    grad_back = back(grad_all)
    norm_back = back(log_norms)
    delta_back = back(delta)

    def query_block(block):
        start = (block * S_DEV).astype(jnp.int32)
        query_pos = start + jnp.arange(S_DEV, dtype=jnp.int32)
        key_pos = start - span + jnp.arange(width, dtype=jnp.int32)
        alive = alive_mask(doc_ends, query_pos, key_pos)
        terms = tile_terms(lax.dynamic_slice_in_dim(query_all, start, S_DEV, 0), lax.dynamic_slice_in_dim(key_front, start, width, 0), lax.dynamic_slice_in_dim(value_front, start, width, 0), lax.dynamic_slice_in_dim(grad_all, start, S_DEV, 0), lax.dynamic_slice_in_dim(log_norms, start, S_DEV, 0), lax.dynamic_slice_in_dim(delta, start, S_DEV, 0), alive)
        return terms[0]

    def key_block(block):
        start = (block * S_DEV).astype(jnp.int32)
        key_pos = start + jnp.arange(S_DEV, dtype=jnp.int32)
        query_pos = start + jnp.arange(width, dtype=jnp.int32)
        alive = alive_mask(doc_ends, query_pos, key_pos)
        terms = tile_terms(lax.dynamic_slice_in_dim(query_back, start, width, 0), lax.dynamic_slice_in_dim(key_all, start, S_DEV, 0), lax.dynamic_slice_in_dim(value_all, start, S_DEV, 0), lax.dynamic_slice_in_dim(grad_back, start, width, 0), lax.dynamic_slice_in_dim(norm_back, start, width, 0), lax.dynamic_slice_in_dim(delta_back, start, width, 0), alive)
        return (terms[1], terms[2])
    blocks = jnp.arange(N_CTX, dtype=jnp.int32)
    grad_queries = lax.map(query_block, blocks)
    grad_keys, grad_values = lax.map(key_block, blocks)
    shape = (TOKENS, HEADS * HD)
    return (grad_queries.reshape(shape).astype(jnp.bfloat16), grad_keys.reshape(shape).astype(jnp.bfloat16), grad_values.reshape(shape).astype(jnp.bfloat16))
```

```python
import math

import jax
import jax.numpy as jnp
from jax import lax
from jax.experimental import pallas as pl
from jax.experimental.pallas import tpu as pltpu
from jax.sharding import PartitionSpec as P

MESH = pl.DeviceIdType.MESH
HD = 128
X, HEAD, Z = 4, 8, 8
PLANE = X * HEAD
ROWS = 64
SPAN = PLANE * ROWS
HALO = SPAN // 2
WIDE = SPAN + HALO
EXTRA = 8
TILE = 256
N_TILE = WIDE // TILE
LOG2E = math.log2(math.e)


def place():
    ctx, head = lax.axis_index("ctx"), lax.axis_index("head")
    z, x = ctx // X, ctx % X
    return z, x, head, x * HEAD + head


def extra_owner(e):
    x = e // 2
    return x * HEAD + (2 * (e % 2) + x % 2) * 2


def own_extra(x, head):
    y, core = head // 2, head % 2
    return (core == 0) & ((x + y) % 2 == 0), x * 2 + y // 2


def plane_device(z, peer):
    return {"ctx": z * X + peer // HEAD, "head": peer % HEAD}


def columns(head):
    return pl.ds(pl.multiple_of(head * HD, HD), HD)


def rows(base, peer):
    return pl.ds(pl.multiple_of(base + peer * ROWS, ROWS), ROWS)


def remote(src, dst, send, recv, device):
    pltpu.make_async_remote_copy(
        src_ref=src, dst_ref=dst, send_sem=send, recv_sem=recv, device_id=device, device_id_type=MESH
    ).start()


def await_bytes(ref, sem):
    pltpu.make_async_copy(ref, ref, sem).wait()


def gather_kernel(
    q_in, k_in, v_in, g_in, lse_in, delta_in,
    q_out, k_out, v_out, g_out, lse_out, delta_out,
    send_sem, stat_send, recv_sem, z_send, z_recv, stat_recv,
):
    z, x, head, p = place()
    owner, e_own = own_extra(x, head)
    lower = p < PLANE // 2
    up = {"ctx": ((z + 1) % Z) * X + x, "head": head}
    down = {"ctx": ((z + Z - 1) % Z) * X + x, "head": head}

    for j in range(5):
        h = head * 5 + j
        slot = h // PLANE
        target = jnp.where(h < PLANE, h, extra_owner(h - PLANE))
        src, dst = lse_in.at[j], lse_out.at[slot, x]

        @pl.when(target == p)
        def _():
            pltpu.make_async_copy(src, dst, stat_recv.at[0, slot]).start()

        @pl.when(target != p)
        def _():
            remote(src, dst, stat_send.at[j], stat_recv.at[0, slot], plane_device(z, target))

    def delta_main(i, carry):
        peer = (p + i) % PLANE
        remote(delta_in.at[peer], delta_out.at[0, p], stat_send.at[5], stat_recv.at[1, 0], plane_device(z, peer))
        return carry

    lax.fori_loop(1, PLANE, delta_main, 0)
    pltpu.make_async_copy(delta_in.at[p], delta_out.at[0, p], stat_recv.at[1, 0]).start()

    def delta_extra(e, carry):
        peer = extra_owner(e)
        src, dst = delta_in.at[PLANE + e], delta_out.at[1, p]

        @pl.when(peer == p)
        def _():
            pltpu.make_async_copy(src, dst, stat_recv.at[1, 1]).start()

        @pl.when(peer != p)
        def _():
            remote(src, dst, stat_send.at[6], stat_recv.at[1, 1], plane_device(z, peer))

        return carry

    lax.fori_loop(0, EXTRA, delta_extra, 0)

    query_side = ((0, q_in, q_out, 0), (3, g_in, g_out, 0))
    key_side = ((1, k_in, k_out, HALO), (2, v_in, v_out, HALO))

    def scatter(side, group):
        def main(i, carry):
            peer = (p + i) % PLANE
            for n, src, dst, base in side:
                remote(
                    src.at[:, columns(peer)], dst.at[0, rows(base, p)],
                    send_sem.at[0, n], recv_sem.at[0, group], plane_device(z, peer),
                )
            return carry

        lax.fori_loop(1, PLANE, main, 0)
        for n, src, dst, base in side:
            pltpu.make_async_copy(src.at[:, columns(p)], dst.at[0, rows(base, p)], recv_sem.at[0, group]).start()

        def extra(i, carry):
            e = (x * 2 + i) % EXTRA
            peer = extra_owner(e)
            for n, src, dst, base in side:
                from_, to = src.at[:, columns(PLANE + e)], dst.at[1, rows(base, p)]

                @pl.when(peer == p)
                def _():
                    pltpu.make_async_copy(from_, to, recv_sem.at[1, group]).start()

                @pl.when(peer != p)
                def _():
                    remote(from_, to, send_sem.at[1, n], recv_sem.at[1, group], plane_device(z, peer))

            return carry

        lax.fori_loop(0, EXTRA, extra, 0)

    @pl.when(lower)
    def _():
        scatter(query_side, 1)
        scatter(key_side, 2)

    @pl.when(jnp.logical_not(lower))
    def _():
        scatter(key_side, 0)
        scatter(query_side, 2)

    high, low, tail = pl.ds(HALO + SPAN - HALO, HALO), pl.ds(0, HALO), pl.ds(SPAN, HALO)

    def forward(slot):
        await_bytes(k_out.at[slot, pl.ds(0, 2 * HALO)], recv_sem.at[slot, 0])
        remote(k_out.at[slot, high], k_out.at[slot, low], z_send.at[slot, 0], z_recv.at[slot, 0], up)
        remote(v_out.at[slot, high], v_out.at[slot, low], z_send.at[slot, 1], z_recv.at[slot, 1], up)
        await_bytes(q_out.at[slot, pl.ds(0, 2 * HALO)], recv_sem.at[slot, 1])
        remote(q_out.at[slot, low], q_out.at[slot, tail], z_send.at[slot, 2], z_recv.at[slot, 2], down)
        remote(g_out.at[slot, low], g_out.at[slot, tail], z_send.at[slot, 3], z_recv.at[slot, 3], down)
        await_bytes(lse_out.at[slot, pl.ds(0, X)], stat_recv.at[0, slot])
        await_bytes(delta_out.at[slot, pl.ds(0, PLANE)], stat_recv.at[1, slot])
        remote(lse_out.at[slot, pl.ds(0, 2)], lse_out.at[slot, pl.ds(X, 2)], z_send.at[slot, 4], z_recv.at[slot, 4], down)
        remote(
            delta_out.at[slot, pl.ds(0, PLANE // 2)], delta_out.at[slot, pl.ds(PLANE, PLANE // 2)],
            z_send.at[slot, 5], z_recv.at[slot, 5], down,
        )

    def finish(slot):
        await_bytes(k_out.at[:, pl.ds(0, 2 * HALO)], recv_sem.at[slot, 2])
        for n, src, dst in (
            (0, k_out.at[slot, high], k_out.at[slot, low]),
            (1, v_out.at[slot, high], v_out.at[slot, low]),
            (2, q_out.at[slot, low], q_out.at[slot, tail]),
            (3, g_out.at[slot, low], g_out.at[slot, tail]),
            (4, lse_out.at[slot, pl.ds(0, 2)], lse_out.at[slot, pl.ds(X, 2)]),
            (5, delta_out.at[slot, pl.ds(0, PLANE // 2)], delta_out.at[slot, pl.ds(PLANE, PLANE // 2)]),
        ):
            await_bytes(src, z_send.at[slot, n])
            await_bytes(dst, z_recv.at[slot, n])

    forward(0)

    @pl.when(owner)
    def _():
        forward(1)

    finish(0)

    @pl.when(owner)
    def _():
        finish(1)

    for j in range(5):
        h = head * 5 + j
        target = jnp.where(h < PLANE, h, extra_owner(h - PLANE))

        @pl.when(target != p)
        def _():
            await_bytes(lse_in.at[j], stat_send.at[j])

    await_bytes(delta_in.at[pl.ds(0, PLANE - 1)], stat_send.at[5])
    for n in range(4):
        await_bytes(k_out.at[0, pl.ds(0, (PLANE - 1) * ROWS)], send_sem.at[0, n])

    @pl.when(owner)
    def _():
        await_bytes(delta_in.at[pl.ds(0, EXTRA - 1)], stat_send.at[6])
        for n in range(4):
            await_bytes(k_out.at[0, pl.ds(0, (EXTRA - 1) * ROWS)], send_sem.at[1, n])

    @pl.when(jnp.logical_not(owner))
    def _():
        await_bytes(delta_in.at[pl.ds(0, EXTRA)], stat_send.at[6])
        for n in range(4):
            await_bytes(k_out.at[0, pl.ds(0, EXTRA * ROWS)], send_sem.at[1, n])


def gather(q, k, v, g, lse, delta):
    wide = jax.ShapeDtypeStruct((2, WIDE, HD), jnp.bfloat16)
    return pl.pallas_call(
        gather_kernel,
        name="gather_heads",
        out_shape=(
            wide, wide, wide, wide,
            jax.ShapeDtypeStruct((2, 6, 4, 128), jnp.float32),
            jax.ShapeDtypeStruct((2, PLANE + PLANE // 2, 1, 128), jnp.float32),
        ),
        in_specs=[pl.BlockSpec(memory_space=pl.ANY)] * 6,
        out_specs=[pl.BlockSpec(memory_space=pl.ANY)] * 6,
        scratch_shapes=[
            pltpu.SemaphoreType.DMA((2, 4)),
            pltpu.SemaphoreType.DMA((7,)),
            pltpu.SemaphoreType.DMA((2, 3)),
            pltpu.SemaphoreType.DMA((2, 6)),
            pltpu.SemaphoreType.DMA((2, 6)),
            pltpu.SemaphoreType.DMA((2, 2)),
        ],
        compiler_params=pltpu.CompilerParams(has_side_effects=True),
    )(q, k, v, g, lse, delta)


def attention_kernel(
    info, q_ref, k_ref, v_ref, g_ref, lse_ref, delta_ref, start_ref, dq_ref, dk_ref, dv_ref, dq_acc, dk_acc, dv_acc
):
    scaling = 1.0 / math.sqrt(HD)
    own = info[4 * N_TILE]

    @pl.when((pl.program_id(0) == 0) | (own > 0))
    def _():
        dq_acc[...] = jnp.zeros_like(dq_acc)

        def key_tile(j, carry):
            key_rows = pl.ds(pl.multiple_of(j * TILE, TILE), TILE)
            key, value = k_ref[0, key_rows], v_ref[0, key_rows]
            key_t = key.T
            dk_acc[...] = jnp.zeros_like(dk_acc)
            dv_acc[...] = jnp.zeros_like(dv_acc)
            key_pos = j * TILE - HALO + lax.broadcasted_iota(jnp.int32, (TILE, 1), 0)

            def pair(i, masked):
                query_rows = pl.ds(pl.multiple_of(i * TILE, TILE), TILE)
                query, grad = q_ref[0, query_rows], g_ref[0, query_rows]
                score = lax.dot_general(key, query, (((1,), (1,)), ((), ())), preferred_element_type=jnp.float32)
                weight = jnp.exp2(score * (scaling * LOG2E) - lse_ref[0, i])
                if masked:
                    query_pos = i * TILE + lax.broadcasted_iota(jnp.int32, (1, TILE), 1)
                    weight = jnp.where((key_pos <= query_pos) & (key_pos >= start_ref[i]), weight, 0.0)
                dweight = lax.dot_general(value, grad, (((1,), (1,)), ((), ())), preferred_element_type=jnp.float32)
                dscore = (weight * (dweight - delta_ref[0, i])).astype(jnp.bfloat16)
                dv_acc[...] += jnp.dot(weight.astype(jnp.bfloat16), grad, preferred_element_type=jnp.float32)
                dk_acc[...] += jnp.dot(dscore, query, preferred_element_type=jnp.float32)
                dq_acc[i] += jnp.dot(key_t, dscore, preferred_element_type=jnp.float32)

            def loop(low, high, masked):
                def step(i, carry):
                    pair(i, masked)
                    return carry

                lax.fori_loop(low, high, step, 0)

            loop(info[4 * j], info[4 * j + 1], True)
            loop(info[4 * j + 1], info[4 * j + 2], False)
            loop(info[4 * j + 2], info[4 * j + 3], True)
            dk_ref[0, key_rows] = (dk_acc[...] * scaling).astype(jnp.bfloat16)
            dv_ref[0, key_rows] = dv_acc[...].astype(jnp.bfloat16)
            return carry

        lax.fori_loop(0, N_TILE, key_tile, 0)

        def store(i, carry):
            dq_ref[0, pl.ds(pl.multiple_of(i * TILE, TILE), TILE)] = (dq_acc[i] * scaling).T.astype(jnp.bfloat16)
            return carry

        lax.fori_loop(0, N_TILE, store, 0)


def attention(info, q, k, v, g, lse, delta, start):
    def slot(s, info):
        return s * info[4 * N_TILE]

    wide = pl.BlockSpec((1, WIDE, HD), lambda s, info: (slot(s, info), 0, 0))
    stat = pl.BlockSpec((1, N_TILE, 1, TILE), lambda s, info: (slot(s, info), 0, 0, 0))
    shape = jax.ShapeDtypeStruct((2, WIDE, HD), jnp.bfloat16)
    return pl.pallas_call(
        attention_kernel,
        name="attention_backward",
        out_shape=(shape, shape, shape),
        grid_spec=pltpu.PrefetchScalarGridSpec(
            num_scalar_prefetch=1,
            grid=(2,),
            in_specs=[wide, wide, wide, wide, stat, stat, pl.BlockSpec((N_TILE, 1, TILE), lambda s, info: (0, 0, 0))],
            out_specs=[wide, wide, wide],
            scratch_shapes=[
                pltpu.VMEM((N_TILE, HD, TILE), jnp.float32),
                pltpu.VMEM((TILE, HD), jnp.float32),
                pltpu.VMEM((TILE, HD), jnp.float32),
            ],
        ),
        compiler_params=pltpu.CompilerParams(vmem_limit_bytes=40 * 2**20),
    )(info, q, k, v, g, lse, delta, start)


def scatter_kernel(
    dq_in, dk_in, dv_in, dq_out, dk_out, dv_out, halo, part, total, send_sem, recv_sem, z_send, z_recv, load_sem
):
    z, x, head, p = place()
    owner, e_own = own_extra(x, head)
    up = {"ctx": ((z + 1) % Z) * X + x, "head": head}
    down = {"ctx": ((z + Z - 1) % Z) * X + x, "head": head}
    half = PLANE // 2
    ins, outs, bases = (dq_in, dk_in, dv_in), (dq_out, dk_out, dv_out), (0, HALO, HALO)
    sent = (pl.ds(SPAN, HALO), pl.ds(0, HALO), pl.ds(0, HALO))
    kept = (pl.ds(0, HALO), pl.ds(SPAN, HALO), pl.ds(SPAN, HALO))

    def exchange(slot):
        for n, device in ((1, down), (2, down), (0, up)):
            remote(ins[n].at[slot, sent[n]], halo.at[slot, n], z_send.at[slot, n], z_recv.at[slot, n], device)
        for n in range(3):
            pltpu.make_async_copy(ins[n].at[slot, kept[n]], part.at[slot, n], load_sem.at[slot, n]).start()

    def deliver(slot, at, n, src, peer):
        dst = outs[n].at[:, columns(at)]

        @pl.when(peer == p)
        def _():
            pltpu.make_async_copy(src, dst, recv_sem.at[n]).start()

        @pl.when(peer != p)
        def _():
            remote(src, dst, send_sem.at[slot, n], recv_sem.at[n], plane_device(z, peer))

    def early(slot, at):
        def step(i, carry):
            low, high = (p + i) % half, half + (p + i) % half
            for n, peer in ((1, low), (2, low), (0, high)):
                deliver(slot, at, n, ins[n].at[slot, rows(bases[n], peer)], peer)
            return carry

        lax.fori_loop(0, half, step, 0)

    def combine(slot):
        for n in range(3):
            await_bytes(part.at[slot, n], load_sem.at[slot, n])
            await_bytes(halo.at[slot, n], z_recv.at[slot, n])
            total[slot, n] = (part[slot, n].astype(jnp.float32) + halo[slot, n].astype(jnp.float32)).astype(jnp.bfloat16)

    def late(slot, at):
        def step(i, carry):
            low = (p + i) % half
            for n, peer in ((1, half + low), (2, half + low), (0, low)):
                deliver(slot, at, n, total.at[slot, n, rows(0, low)], peer)
            return carry

        lax.fori_loop(0, half, step, 0)

    def finish(slot):
        for n in range(3):
            await_bytes(halo.at[slot, n], z_send.at[slot, n])
            await_bytes(ins[n].at[slot, pl.ds(0, (PLANE - 1) * ROWS)], send_sem.at[slot, n])

    exchange(0)

    @pl.when(owner)
    def _():
        exchange(1)

    early(0, p)

    @pl.when(owner)
    def _():
        early(1, PLANE + e_own)

    combine(0)
    late(0, p)

    @pl.when(owner)
    def _():
        combine(1)
        late(1, PLANE + e_own)

    for n in range(3):
        await_bytes(outs[n], recv_sem.at[n])
    finish(0)

    @pl.when(owner)
    def _():
        finish(1)


def scatter(dq, dk, dv):
    shape = jax.ShapeDtypeStruct((ROWS, (PLANE + EXTRA) * HD), jnp.bfloat16)
    buffer = pltpu.VMEM((2, 3, HALO, HD), jnp.bfloat16)
    return pl.pallas_call(
        scatter_kernel,
        name="scatter_heads",
        out_shape=(shape, shape, shape),
        in_specs=[pl.BlockSpec(memory_space=pl.ANY)] * 3,
        out_specs=[pl.BlockSpec(memory_space=pl.ANY)] * 3,
        scratch_shapes=[
            buffer, buffer, buffer,
            pltpu.SemaphoreType.DMA((2, 3)),
            pltpu.SemaphoreType.DMA((3,)),
            pltpu.SemaphoreType.DMA((2, 3)),
            pltpu.SemaphoreType.DMA((2, 3)),
            pltpu.SemaphoreType.DMA((2, 3)),
        ],
        compiler_params=pltpu.CompilerParams(has_side_effects=True, vmem_limit_bytes=32 * 2**20),
    )(dq, dk, dv)


def plan(doc_lengths):
    z, x, head, _ = place()
    owner, _ = own_extra(x, head)
    ends = jnp.cumsum(doc_lengths) - z * SPAN
    starts = ends - doc_lengths

    def start_of(pos):
        return jnp.max(jnp.where(starts[None, :] <= pos[:, None], starts[None, :], -(1 << 20)), axis=1)

    def end_of(pos):
        return jnp.min(jnp.where(ends[None, :] > pos[:, None], ends[None, :], 1 << 20), axis=1)

    query_start = start_of(jnp.arange(WIDE, dtype=jnp.int32))
    first = jnp.arange(N_TILE, dtype=jnp.int32) * TILE - HALO
    last = first + TILE - 1
    end_first, end_last = end_of(first), end_of(last)
    take_low = jnp.any((starts < 0) & (ends > 0) & (starts >= -HALO))
    take_high = jnp.any((starts < SPAN) & (ends > SPAN) & (starts < SPAN - HALO))
    limit = jnp.where(first < 0, SPAN, jnp.where(take_high, WIDE, SPAN))
    limit = jnp.where((first < 0) & ~take_low, 0, limit)
    low = jnp.maximum(first, 0) // TILE
    high = jnp.maximum((jnp.minimum(end_last, limit) + TILE - 1) // TILE, low)
    full_low = jnp.clip((jnp.maximum(last, 0) + TILE - 1) // TILE, low, high)
    full_high = jnp.clip(jnp.maximum(end_first, 0) // TILE, full_low, high)
    info = jnp.stack([low, full_low, full_high, high], axis=1).reshape(-1)
    info = jnp.concatenate([info, owner.astype(jnp.int32)[None]])
    return info.astype(jnp.int32), query_start.astype(jnp.int32).reshape(N_TILE, 1, TILE)


def on_device(queries, keys, values, outputs, out_grad, log_norms, doc_lengths):
    heads = queries.shape[1] // HD
    product = out_grad.astype(jnp.float32) * outputs.astype(jnp.float32)
    delta = jnp.sum(product.reshape(ROWS, heads, HD), axis=-1)
    delta = jnp.pad(delta.T, ((0, 0), (0, 128 - ROWS))).reshape(heads, 1, 128)
    lse = (log_norms * LOG2E).T.reshape(heads // HEAD, 4, 128)
    q, k, v, g, lse, delta = gather(queries, keys, values, out_grad, lse, delta)
    lse = lse.reshape(2, N_TILE, 1, TILE)
    delta = delta[..., :ROWS].reshape(2, N_TILE, 1, TILE)
    info, query_start = plan(doc_lengths)
    dq, dk, dv = attention(info, q, k, v, g, lse, delta, query_start)
    return scatter(dq, dk, dv)


def solution(mesh):
    row = P(("ctx", "head"), None)
    return jax.shard_map(
        on_device,
        mesh=mesh,
        in_specs=(row, row, row, row, row, P("ctx", "head"), P()),
        out_specs=(row, row, row),
        check_vma=False,
    )
```

```python
import math

import jax
import jax.numpy as jnp
from jax import lax
from jax.experimental import pallas as pl
from jax.experimental.pallas import tpu as pltpu
from jax.sharding import PartitionSpec as P

NT = (((1,), (1,)), ((), ()))
MESH = pl.DeviceIdType.MESH
HD = 128
X, HEAD, Z = 4, 8, 8
PLANE = X * HEAD
ROWS = 64
SPAN = PLANE * ROWS
HALO = SPAN // 2
WIDE = SPAN + HALO
EXTRA = 8
TILE = 256
N_TILE = WIDE // TILE
DOCS = 16
LOG2E = math.log2(math.e)


def place():
    ctx, head = lax.axis_index("ctx"), lax.axis_index("head")
    z, x = ctx // X, ctx % X
    return z, x, head, x * HEAD + head


def extra_owner(e):
    x = e // 2
    return x * HEAD + (2 * (e % 2) + x % 2) * 2


def own_extra(x, head):
    y, core = head // 2, head % 2
    return (core == 0) & ((x + y) % 2 == 0), x * 2 + y // 2


def plane_device(z, peer):
    return {"ctx": z * X + peer // HEAD, "head": peer % HEAD}


def columns(head):
    return pl.ds(pl.multiple_of(head * HD, HD), HD)


def rows(base, peer):
    return pl.ds(pl.multiple_of(base + peer * ROWS, ROWS), ROWS)


def greet(z, x, head, p):
    barrier = pltpu.get_barrier_semaphore()

    def signal(i, carry):
        pl.semaphore_signal(barrier, inc=1, device_id=plane_device(z, (p + i) % PLANE), device_id_type=MESH)
        return carry

    lax.fori_loop(1, PLANE, signal, 0)
    for step in (1, Z - 1):
        pl.semaphore_signal(barrier, inc=1, device_id={"ctx": ((z + step) % Z) * X + x, "head": head}, device_id_type=MESH)
    return barrier


def remote(src, dst, send, recv, device):
    pltpu.make_async_remote_copy(
        src_ref=src, dst_ref=dst, send_sem=send, recv_sem=recv, device_id=device, device_id_type=MESH
    ).start()


def await_bytes(ref, sem):
    pltpu.make_async_copy(ref, ref, sem).wait()


def local_statistics(p, grad, output, norm, lse, delta):
    heads = delta.shape[0]
    product = grad[...].astype(jnp.float32) * output[...].astype(jnp.float32)
    high = product.astype(jnp.bfloat16)
    low = (product - high.astype(jnp.float32)).astype(jnp.bfloat16)
    head_of = lax.broadcasted_iota(jnp.int32, (heads, heads * HD), 1) // HD
    select = jnp.where(head_of == lax.broadcasted_iota(jnp.int32, (heads, heads * HD), 0), 1.0, 0.0).astype(jnp.bfloat16)
    sums = lax.dot_general(select, high, NT, preferred_element_type=jnp.float32)
    sums += lax.dot_general(select, low, NT, preferred_element_type=jnp.float32)
    empty = jnp.zeros_like(sums)
    wide = jnp.where(p % 2 == 0, jnp.concatenate([sums, empty], axis=1), jnp.concatenate([empty, sums], axis=1))
    for h in range(heads):
        delta[h] = wide[h : h + 1]
    for j in range(lse.shape[0]):
        for c in range(4):
            lse[j, pl.ds(c, 1), :] = norm[pl.ds(j, 1), pl.ds(c * 128, 128)]


def gather_kernel(
    q_in, k_in, v_in, g_in, o_in, norm_in,
    q_out, k_out, v_out, g_out, lse_out, delta_out,
    grad, output, norm, lse_in, delta_in,
    send_sem, stat_send, recv_sem, z_send, z_recv, z_stat, stat_recv, load_sem,
):
    z, x, head, p = place()
    owner, e_own = own_extra(x, head)
    barrier = greet(z, x, head, p)
    loads = [
        pltpu.make_async_copy(src, dst, load_sem.at[n])
        for n, (src, dst) in enumerate(((g_in, grad), (o_in, output), (norm_in, norm)))
    ]
    for load in loads:
        load.start()
    for load in loads:
        load.wait()
    local_statistics(p, grad, output, norm, lse_in, delta_in)
    pl.semaphore_wait(barrier, PLANE + 1)
    lower = p < PLANE // 2
    up = {"ctx": ((z + 1) % Z) * X + x, "head": head}
    down = {"ctx": ((z + Z - 1) % Z) * X + x, "head": head}

    for j in range(5):
        h = head * 5 + j
        slot = h // PLANE
        target = jnp.where(h < PLANE, h, extra_owner(h - PLANE))
        src, dst = lse_in.at[j], lse_out.at[slot, x]

        @pl.when(target == p)
        def _():
            pltpu.make_async_copy(src, dst, stat_recv.at[0, slot]).start()

        @pl.when(target != p)
        def _():
            remote(src, dst, stat_send.at[j], stat_recv.at[0, slot], plane_device(z, target))

    def delta_main(i, carry):
        peer = (p + i) % PLANE
        remote(delta_in.at[peer], delta_out.at[0, p], stat_send.at[5], stat_recv.at[1, 0], plane_device(z, peer))
        return carry

    lax.fori_loop(1, PLANE, delta_main, 0)
    pltpu.make_async_copy(delta_in.at[p], delta_out.at[0, p], stat_recv.at[1, 0]).start()

    def delta_extra(e, carry):
        peer = extra_owner(e)
        src, dst = delta_in.at[PLANE + e], delta_out.at[1, p]

        @pl.when(peer == p)
        def _():
            pltpu.make_async_copy(src, dst, stat_recv.at[1, 1]).start()

        @pl.when(peer != p)
        def _():
            remote(src, dst, stat_send.at[6], stat_recv.at[1, 1], plane_device(z, peer))

        return carry

    lax.fori_loop(0, EXTRA, delta_extra, 0)

    query_side = ((0, q_in, q_out, 0), (3, g_in, g_out, 0))
    key_side = ((1, k_in, k_out, HALO), (2, v_in, v_out, HALO))
    rest = X

    def scatter(side, group):
        def step(i, carry):
            peer = (p + i) % PLANE
            for n, src, dst, base in side:
                from_, to = src.at[:, columns(peer)], dst.at[0, rows(base, p)]

                @pl.when(peer == p)
                def _():
                    pltpu.make_async_copy(from_, to, recv_sem.at[0, group]).start()

                @pl.when(peer != p)
                def _():
                    remote(from_, to, send_sem.at[0, n], recv_sem.at[0, group], plane_device(z, peer))

            @pl.when(i % 4 == 0)
            def _():
                e = (x * 2 + i // 4) % EXTRA
                extra = extra_owner(e)
                for n, src, dst, base in side:
                    from_, to = src.at[:, columns(PLANE + e)], dst.at[1, rows(base, p)]

                    @pl.when(extra == p)
                    def _():
                        pltpu.make_async_copy(from_, to, recv_sem.at[1, group]).start()

                    @pl.when(extra != p)
                    def _():
                        remote(from_, to, send_sem.at[1, n], recv_sem.at[1, group], plane_device(z, extra))

            return carry

        lax.fori_loop(0, PLANE, step, 0)

    @pl.when(lower)
    def _():
        scatter(query_side, x)
        scatter(key_side, rest)

    @pl.when(jnp.logical_not(lower))
    def _():
        scatter(key_side, x)
        scatter(query_side, rest)

    block = SPAN // X
    stats = (
        (0, lse_out, pl.ds(0, 2), pl.ds(X, 2)),
        (1, delta_out, pl.ds(0, PLANE // 2), pl.ds(PLANE, PLANE // 2)),
    )

    def forward_stats(slot):
        await_bytes(lse_out.at[slot, pl.ds(0, X)], stat_recv.at[0, slot])
        await_bytes(delta_out.at[slot, pl.ds(0, PLANE)], stat_recv.at[1, slot])
        for n, ref, near, far in stats:
            remote(ref.at[slot, near], ref.at[slot, far], z_stat.at[0, slot, n], z_stat.at[1, slot, n], down)

    def pieces(xs):
        here = pl.ds(pl.multiple_of(HALO + xs * block, block), block)
        there = pl.ds(pl.multiple_of((xs - X // 2) * block, block), block)
        low_here = pl.ds(pl.multiple_of(xs * block, block), block)
        low_there = pl.ds(pl.multiple_of(SPAN + xs * block, block), block)
        return ((k_out, here, there), (v_out, here, there)), ((q_out, low_here, low_there), (g_out, low_here, low_there))

    def forward(slot, xs):
        await_bytes(k_out.at[slot, pl.ds(0, 2 * block)], recv_sem.at[slot, xs])
        keys, queries = pieces(xs)

        @pl.when(xs >= X // 2)
        def _():
            for n, (ref, here, there) in enumerate(keys):
                remote(ref.at[slot, here], ref.at[slot, there], z_send.at[slot, xs, n], z_recv.at[slot, xs, n], up)

        @pl.when(xs < X // 2)
        def _():
            for n, (ref, here, there) in enumerate(queries):
                remote(ref.at[slot, here], ref.at[slot, there], z_send.at[slot, xs, n], z_recv.at[slot, xs, n], down)

    def finish(slot):
        await_bytes(k_out.at[:, pl.ds(0, 2 * HALO)], recv_sem.at[slot, rest])
        for xs in range(X):
            for n in range(2):
                await_bytes(k_out.at[slot, pl.ds(0, block)], z_send.at[slot, xs, n])
                await_bytes(k_out.at[slot, pl.ds(0, block)], z_recv.at[slot, xs, n])
        for n, ref, near, far in stats:
            await_bytes(ref.at[slot, near], z_stat.at[0, slot, n])
            await_bytes(ref.at[slot, far], z_stat.at[1, slot, n])

    for d in (1, 2, 3, 0):
        xs = (x + X - d) % X
        forward(0, xs)

        @pl.when(owner)
        def _():
            forward(1, xs)

    forward_stats(0)

    @pl.when(owner)
    def _():
        forward_stats(1)

    finish(0)

    @pl.when(owner)
    def _():
        finish(1)

    for j in range(5):
        h = head * 5 + j
        target = jnp.where(h < PLANE, h, extra_owner(h - PLANE))

        @pl.when(target != p)
        def _():
            await_bytes(lse_in.at[j], stat_send.at[j])

    await_bytes(delta_in.at[pl.ds(0, PLANE - 1)], stat_send.at[5])
    for n in range(4):
        await_bytes(k_out.at[0, pl.ds(0, (PLANE - 1) * ROWS)], send_sem.at[0, n])

    @pl.when(owner)
    def _():
        await_bytes(delta_in.at[pl.ds(0, EXTRA - 1)], stat_send.at[6])
        for n in range(4):
            await_bytes(k_out.at[0, pl.ds(0, (EXTRA - 1) * ROWS)], send_sem.at[1, n])

    @pl.when(jnp.logical_not(owner))
    def _():
        await_bytes(delta_in.at[pl.ds(0, EXTRA)], stat_send.at[6])
        for n in range(4):
            await_bytes(k_out.at[0, pl.ds(0, EXTRA * ROWS)], send_sem.at[1, n])


def gather(q, k, v, g, o, norm):
    wide = pltpu.VMEM((2, WIDE, HD), jnp.bfloat16)
    heads = PLANE + EXTRA
    q, k, v, g, o, norm = (pltpu.with_memory_space_constraint(a, pltpu.HBM) for a in (q, k, v, g, o, norm))
    return pl.pallas_call(
        gather_kernel,
        name="gather_heads",
        out_shape=(
            wide, wide, wide, wide,
            pltpu.VMEM((2, 6, 4, 128), jnp.float32),
            pltpu.VMEM((2, PLANE + PLANE // 2, 1, 128), jnp.float32),
        ),
        in_specs=[pl.BlockSpec(memory_space=pltpu.HBM)] * 6,
        out_specs=[pl.BlockSpec(memory_space=pltpu.VMEM)] * 6,
        scratch_shapes=[
            pltpu.VMEM(g.shape, g.dtype),
            pltpu.VMEM(o.shape, o.dtype),
            pltpu.VMEM(norm.shape, norm.dtype),
            pltpu.VMEM((heads // HEAD, 4, 128), jnp.float32),
            pltpu.VMEM((heads, 1, 128), jnp.float32),
            pltpu.SemaphoreType.DMA((2, 4)),
            pltpu.SemaphoreType.DMA((7,)),
            pltpu.SemaphoreType.DMA((2, X + 1)),
            pltpu.SemaphoreType.DMA((2, X, 2)),
            pltpu.SemaphoreType.DMA((2, X, 2)),
            pltpu.SemaphoreType.DMA((2, 2, 2)),
            pltpu.SemaphoreType.DMA((2, 2)),
            pltpu.SemaphoreType.DMA((3,)),
        ],
        compiler_params=pltpu.CompilerParams(has_side_effects=True, collective_id=0, vmem_limit_bytes=24 * 2**20),
    )(q, k, v, g, o, norm)


def prepare(z, lengths, plan, start_t):
    starts, ends, at = [], [], -z * SPAN
    for d in range(DOCS):
        starts.append(at)
        at = at + lengths[d]
        ends.append(at)
    take_low, take_high = jnp.int32(0), jnp.int32(0)
    for start, end in zip(starts, ends):
        take_low = take_low | ((start < 0) & (end > 0) & (start >= -HALO)).astype(jnp.int32)
        take_high = take_high | ((start < SPAN) & (end > SPAN) & (start < SPAN - HALO)).astype(jnp.int32)
    for j in range(N_TILE):
        first = j * TILE - HALO
        last = first + TILE - 1
        end_first = end_last = jnp.int32(1 << 20)
        for end in reversed(ends):
            end_first = jnp.where(end > first, end, end_first)
            end_last = jnp.where(end > last, end, end_last)
        limit = jnp.where(take_low > 0, SPAN, 0) if first < 0 else jnp.where(take_high > 0, WIDE, SPAN)
        low = jnp.int32(max(first, 0) // TILE)
        high = jnp.maximum((jnp.maximum(jnp.minimum(end_last, limit), 0) + TILE - 1) // TILE, low)
        full_low = jnp.clip(jnp.int32((max(last, 0) + TILE - 1) // TILE), low, high)
        full_high = jnp.clip(jnp.maximum(end_first, 0) // TILE, full_low, high)
        for n, value in enumerate((low, full_low, full_high, high)):
            plan[4 * j + n] = value
    for i in range(N_TILE):
        pos = i * TILE + lax.broadcasted_iota(jnp.int32, (1, TILE), 1)
        own = jnp.full((1, TILE), -(1 << 20), jnp.int32)
        for start in starts:
            own = jnp.where(pos >= start, start, own)
        start_t[i] = own


def attention_kernel(
    lengths, q_ref, k_ref, v_ref, g_ref, lse_ref, delta_ref, dq_ref, dk_ref, dv_ref,
    dq_acc, dk_acc, dv_acc, lse_t, delta_t, start_t, plan,
):
    scaling = 1.0 / math.sqrt(HD)

    def run(slots):
        for s in slots:
            for i in range(N_TILE):
                lse, delta = [], []
                for c in range(2 * i, 2 * i + 2):
                    lse.append(lse_ref[s, c // 4, pl.ds(c % 4, 1), :] * LOG2E)
                    delta.append(delta_ref[s, 2 * c] + delta_ref[s, 2 * c + 1])
                lse_t[s, i] = jnp.concatenate(lse, axis=1)
                delta_t[s, i] = jnp.concatenate(delta, axis=1)
            dq_acc[s] = jnp.zeros(dq_acc.shape[1:], jnp.float32)

        def key_tile(j, carry):
            key_rows = pl.ds(pl.multiple_of(j * TILE, TILE), TILE)

            @pl.when(plan[4 * j + 3] <= plan[4 * j])
            def _():
                for s in slots:
                    dk_ref[s, key_rows] = jnp.zeros((TILE, HD), jnp.bfloat16)
                    dv_ref[s, key_rows] = jnp.zeros((TILE, HD), jnp.bfloat16)

            @pl.when(plan[4 * j + 3] > plan[4 * j])
            def _():
                for s in slots:
                    dk_acc[s] = jnp.zeros((TILE, HD), jnp.float32)
                    dv_acc[s] = jnp.zeros((TILE, HD), jnp.float32)
                key_pos = j * TILE - HALO + lax.broadcasted_iota(jnp.int32, (TILE, 1), 0)
                keys = [k_ref[s, key_rows] for s in slots]
                values = [v_ref[s, key_rows] for s in slots]
                keys_t = [key.T for key in keys]

                def pair(i, masked):
                    query_rows = pl.ds(pl.multiple_of(i * TILE, TILE), TILE)
                    if masked:
                        query_pos = i * TILE + lax.broadcasted_iota(jnp.int32, (1, TILE), 1)
                        live = (key_pos <= query_pos) & (key_pos >= start_t[i])
                    raw = [
                        (
                            lax.dot_general(keys[s], q_ref[s, query_rows], NT, preferred_element_type=jnp.float32),
                            lax.dot_general(values[s], g_ref[s, query_rows], NT, preferred_element_type=jnp.float32),
                        )
                        for s in slots
                    ]
                    low = []
                    for s in slots:
                        score, dweight = raw[s]
                        weight = jnp.exp2(score * (scaling * LOG2E) - lse_t[s, i])
                        if masked:
                            weight = jnp.where(live, weight, 0.0)
                        dscore = weight * (dweight - delta_t[s, i])
                        low.append((weight.astype(jnp.bfloat16), dscore.astype(jnp.bfloat16)))
                    for s in slots:
                        weight, dscore = low[s]
                        dv_acc[s] += jnp.dot(weight, g_ref[s, query_rows], preferred_element_type=jnp.float32)
                        dk_acc[s] += jnp.dot(dscore, q_ref[s, query_rows], preferred_element_type=jnp.float32)
                        dq_acc[s, i] += jnp.dot(keys_t[s], dscore, preferred_element_type=jnp.float32)

                def loop(low, high, masked):
                    def step(i, carry):
                        pair(i, masked)
                        return carry

                    lax.fori_loop(low, high, step, 0)

                loop(plan[4 * j], plan[4 * j + 1], True)
                loop(plan[4 * j + 1], plan[4 * j + 2], False)
                loop(plan[4 * j + 2], plan[4 * j + 3], True)
                for s in slots:
                    dk_ref[s, key_rows] = (dk_acc[s] * scaling).astype(jnp.bfloat16)
                    dv_ref[s, key_rows] = dv_acc[s].astype(jnp.bfloat16)

            return carry

        lax.fori_loop(0, N_TILE, key_tile, 0)
        for s in slots:

            def store(i, carry):
                query_rows = pl.ds(pl.multiple_of(i * TILE, TILE), TILE)
                dq_ref[s, query_rows] = (dq_acc[s, i] * scaling).T.astype(jnp.bfloat16)
                return carry

            lax.fori_loop(0, N_TILE, store, 0)

    z, x, head, _ = place()
    owner, _ = own_extra(x, head)
    prepare(z, lengths, plan, start_t)

    @pl.when(owner)
    def _():
        run((0, 1))

    @pl.when(jnp.logical_not(owner))
    def _():
        run((0,))


def attention(lengths, q, k, v, g, lse, delta):
    shape = pltpu.VMEM((2, WIDE, HD), jnp.bfloat16)
    whole = pl.BlockSpec(memory_space=pltpu.VMEM)
    return pl.pallas_call(
        attention_kernel,
        name="attention_backward",
        out_shape=(shape, shape, shape),
        in_specs=[pl.BlockSpec(memory_space=pltpu.SMEM)] + [whole] * 6,
        out_specs=[whole] * 3,
        scratch_shapes=[
            pltpu.VMEM((2, N_TILE, HD, TILE), jnp.float32),
            pltpu.VMEM((2, TILE, HD), jnp.float32),
            pltpu.VMEM((2, TILE, HD), jnp.float32),
            pltpu.VMEM((2, N_TILE, 1, TILE), jnp.float32),
            pltpu.VMEM((2, N_TILE, 1, TILE), jnp.float32),
            pltpu.VMEM((N_TILE, 1, TILE), jnp.int32),
            pltpu.SMEM((4 * N_TILE,), jnp.int32),
        ],
        compiler_params=pltpu.CompilerParams(vmem_limit_bytes=24 * 2**20),
    )(lengths, q, k, v, g, lse, delta)


def scatter_kernel(
    dq_in, dk_in, dv_in, dq_out, dk_out, dv_out, halo, part, total, send_sem, recv_sem, z_send, z_recv, load_sem
):
    z, x, head, p = place()
    owner, e_own = own_extra(x, head)
    up = {"ctx": ((z + 1) % Z) * X + x, "head": head}
    down = {"ctx": ((z + Z - 1) % Z) * X + x, "head": head}
    barrier = greet(z, x, head, p)
    half = PLANE // 2
    ins, outs, bases = (dq_in, dk_in, dv_in), (dq_out, dk_out, dv_out), (0, HALO, HALO)
    sent = (pl.ds(SPAN, HALO), pl.ds(0, HALO), pl.ds(0, HALO))
    kept = (pl.ds(0, HALO), pl.ds(SPAN, HALO), pl.ds(SPAN, HALO))

    def exchange(slot):
        for n, device in ((1, down), (0, up), (2, down)):
            remote(ins[n].at[slot, sent[n]], halo.at[slot, n], z_send.at[slot, n], z_recv.at[slot, n], device)
        for n in range(3):
            pltpu.make_async_copy(ins[n].at[slot, kept[n]], part.at[slot, n], load_sem.at[slot, n]).start()

    def deliver(slot, at, n, src, peer):
        dst = outs[n].at[:, columns(at)]

        @pl.when(peer == p)
        def _():
            pltpu.make_async_copy(src, dst, recv_sem.at[n]).start()

        @pl.when(peer != p)
        def _():
            remote(src, dst, send_sem.at[slot, n], recv_sem.at[n], plane_device(z, peer))

    def early(slot, at):
        def step(i, carry):
            low, high = (p + i) % half, half + (p + i) % half
            for n, peer in ((1, low), (2, low), (0, high)):
                deliver(slot, at, n, ins[n].at[slot, rows(bases[n], peer)], peer)
            return carry

        lax.fori_loop(0, half, step, 0)

    def late(slot, at, n):
        await_bytes(part.at[slot, n], load_sem.at[slot, n])
        await_bytes(halo.at[slot, n], z_recv.at[slot, n])
        total[slot, n] = (part[slot, n].astype(jnp.float32) + halo[slot, n].astype(jnp.float32)).astype(jnp.bfloat16)

        def step(i, carry):
            low = (p + i) % half
            deliver(slot, at, n, total.at[slot, n, rows(0, low)], low if n == 0 else half + low)
            return carry

        lax.fori_loop(0, half, step, 0)

    def finish(slot):
        for n in range(3):
            await_bytes(halo.at[slot, n], z_send.at[slot, n])
            await_bytes(ins[n].at[slot, pl.ds(0, (PLANE - 1) * ROWS)], send_sem.at[slot, n])

    pl.semaphore_wait(barrier, PLANE + 1)
    exchange(0)

    @pl.when(owner)
    def _():
        exchange(1)

    early(0, p)

    @pl.when(owner)
    def _():
        early(1, PLANE + e_own)

    for n in (1, 0, 2):
        late(0, p, n)

        @pl.when(owner)
        def _():
            late(1, PLANE + e_own, n)

    for n in range(3):
        await_bytes(outs[n], recv_sem.at[n])
    finish(0)

    @pl.when(owner)
    def _():
        finish(1)


def scatter(dq, dk, dv):
    shape = jax.ShapeDtypeStruct((ROWS, (PLANE + EXTRA) * HD), jnp.bfloat16)
    buffer = pltpu.VMEM((2, 3, HALO, HD), jnp.bfloat16)
    return pl.pallas_call(
        scatter_kernel,
        name="scatter_heads",
        out_shape=(shape, shape, shape),
        in_specs=[pl.BlockSpec(memory_space=pl.ANY)] * 3,
        out_specs=[pl.BlockSpec(memory_space=pl.ANY)] * 3,
        scratch_shapes=[
            buffer, buffer, buffer,
            pltpu.SemaphoreType.DMA((2, 3)),
            pltpu.SemaphoreType.DMA((3,)),
            pltpu.SemaphoreType.DMA((2, 3)),
            pltpu.SemaphoreType.DMA((2, 3)),
            pltpu.SemaphoreType.DMA((2, 3)),
        ],
        compiler_params=pltpu.CompilerParams(has_side_effects=True, collective_id=1, vmem_limit_bytes=24 * 2**20),
    )(dq, dk, dv)


def on_device(queries, keys, values, outputs, out_grad, log_norms, doc_lengths):
    q, k, v, g, lse, delta = gather(queries, keys, values, out_grad, outputs, log_norms.T)
    dq, dk, dv = attention(doc_lengths, q, k, v, g, lse, delta)
    return scatter(dq, dk, dv)


def solution(mesh):
    row = P(("ctx", "head"), None)
    return jax.shard_map(
        on_device,
        mesh=mesh,
        in_specs=(row, row, row, row, row, P("ctx", "head"), P()),
        out_specs=(row, row, row),
        check_vma=False,
    )
```

```python
import math

import jax
import jax.numpy as jnp
from jax import lax
from jax.experimental import pallas as pl
from jax.experimental.pallas import tpu as pltpu
from jax.sharding import PartitionSpec as P

NT = (((1,), (1,)), ((), ()))
MESH = pl.DeviceIdType.MESH
HD = 128
X, HEAD, Z = 4, 8, 8
PLANE = X * HEAD
ROWS = 64
SPAN = PLANE * ROWS
HALO = SPAN // 2
WIDE = SPAN + HALO
EXTRA = 8
TILE = 256
N_TILE = WIDE // TILE
AT_ONCE = 3
DOCS = 16
LOG2E = math.log2(math.e)


def place():
    ctx, head = lax.axis_index("ctx"), lax.axis_index("head")
    z, x = ctx // X, ctx % X
    return z, x, head, x * HEAD + head


def extra_owner(e):
    x = e // 2
    return x * HEAD + (2 * (e % 2) + x % 2) * 2


def own_extra(x, head):
    y, core = head // 2, head % 2
    return (core == 0) & ((x + y) % 2 == 0), x * 2 + y // 2


def plane_device(z, peer):
    return {"ctx": z * X + peer // HEAD, "head": peer % HEAD}


def turn(i):
    return (2 + 4 * (i % 2) + 2 * (i // 2 % 2) + i // 4) % HEAD


def columns(head):
    return pl.ds(pl.multiple_of(head * HD, HD), HD)


def rows(base, peer):
    return pl.ds(pl.multiple_of(base + peer * ROWS, ROWS), ROWS)


def greet(z, x, head, p):
    barrier = pltpu.get_barrier_semaphore()

    for i in range(1, PLANE):
        pl.semaphore_signal(barrier, inc=1, device_id=plane_device(z, (p + i) % PLANE), device_id_type=MESH)
    for step in (1, Z - 1):
        pl.semaphore_signal(barrier, inc=1, device_id={"ctx": ((z + step) % Z) * X + x, "head": head}, device_id_type=MESH)
    return barrier


def remote(src, dst, send, recv, device):
    pltpu.make_async_remote_copy(
        src_ref=src, dst_ref=dst, send_sem=send, recv_sem=recv, device_id=device, device_id_type=MESH
    ).start()


def await_bytes(ref, sem):
    pltpu.make_async_copy(ref, ref, sem).wait()


def local_statistics(p, grad, output, norm, lse, delta):
    heads = delta.shape[0]
    product = grad[...].astype(jnp.float32) * output[...].astype(jnp.float32)
    high = product.astype(jnp.bfloat16)
    low = (product - high.astype(jnp.float32)).astype(jnp.bfloat16)
    head_of = lax.broadcasted_iota(jnp.int32, (heads, heads * HD), 1) // HD
    select = jnp.where(head_of == lax.broadcasted_iota(jnp.int32, (heads, heads * HD), 0), 1.0, 0.0).astype(jnp.bfloat16)
    sums = lax.dot_general(select, high, NT, preferred_element_type=jnp.float32)
    sums += lax.dot_general(select, low, NT, preferred_element_type=jnp.float32)
    empty = jnp.zeros_like(sums)
    wide = jnp.where(p % 2 == 0, jnp.concatenate([sums, empty], axis=1), jnp.concatenate([empty, sums], axis=1))
    for h in range(heads):
        delta[h] = wide[h : h + 1]
    for j in range(lse.shape[0]):
        for c in range(4):
            lse[j, pl.ds(c, 1), :] = norm[pl.ds(j, 1), pl.ds(c * 128, 128)]


def prepare(z, lengths, plan, start_t):
    starts, ends, at = [], [], -z * SPAN
    for d in range(DOCS):
        starts.append(at)
        at = at + lengths[d]
        ends.append(at)
    take_low, take_high = jnp.int32(0), jnp.int32(0)
    for start, end in zip(starts, ends):
        take_low = take_low | ((start < 0) & (end > 0) & (start >= -HALO)).astype(jnp.int32)
        take_high = take_high | ((start < SPAN) & (end > SPAN) & (start < SPAN - HALO)).astype(jnp.int32)
    for j in range(N_TILE):
        first = j * TILE - HALO
        last = first + TILE - 1
        end_last = jnp.int32(1 << 20)
        for end in reversed(ends):
            end_last = jnp.where(end > last, end, end_last)
        limit = jnp.where(take_low > 0, SPAN, 0) if first < 0 else jnp.where(take_high > 0, WIDE, SPAN)
        low = jnp.int32(max(first, 0) // TILE)
        plan[2 * j] = low
        plan[2 * j + 1] = jnp.maximum((jnp.maximum(jnp.minimum(end_last, limit), 0) + TILE - 1) // TILE, low)
    for i in range(N_TILE):
        pos = i * TILE + lax.broadcasted_iota(jnp.int32, (1, TILE), 1)
        own = jnp.full((1, TILE), -(1 << 20), jnp.int32)
        for start in starts:
            own = jnp.where(pos >= start, start, own)
        start_t[i] = own


def gather_kernel(
    lengths_in, q_in, k_in, v_in, g_in, o_in, norm_in,
    q_out, k_out, v_out, g_out, lse_out, delta_out, start_out, plan_out,
    lengths, grad, output, norm, lse_in, delta_in,
    send_sem, stat_send, recv_sem, z_send, z_recv, z_stat, stat_recv, load_sem,
):
    z, x, head, p = place()
    owner, e_own = own_extra(x, head)
    barrier = greet(z, x, head, p)
    loads = [
        pltpu.make_async_copy(src, dst, load_sem.at[n])
        for n, (src, dst) in enumerate(((g_in, grad), (o_in, output), (norm_in, norm), (lengths_in, lengths)))
    ]
    for load in loads:
        load.start()
    lower = p < PLANE // 2
    up = {"ctx": ((z + 1) % Z) * X + x, "head": head}
    down = {"ctx": ((z + Z - 1) % Z) * X + x, "head": head}
    pl.semaphore_wait(barrier, PLANE + 1)

    query_side = ((0, q_in, q_out, 0), (3, g_in, g_out, 0))
    key_side = ((1, k_in, k_out, HALO), (2, v_in, v_out, HALO))
    rest = X

    def scatter(side, group, away, begin=0, end=HEAD):
        def step(i, carry):
            for d in away:
                to_x = (x + d) % X
                peer = to_x * HEAD + (head + turn(i)) % HEAD
                for n, src, dst, base in side:
                    from_, to = src.at[:, columns(peer)], dst.at[0, rows(base, p)]

                    @pl.when(peer == p)
                    def _():
                        pltpu.make_async_copy(from_, to, recv_sem.at[0, group]).start()

                    @pl.when(peer != p)
                    def _():
                        remote(from_, to, send_sem.at[0, n], recv_sem.at[0, group], plane_device(z, peer))

                @pl.when(i % 4 == 0)
                def _():
                    e = to_x * 2 + i // 4
                    extra = extra_owner(e)
                    for n, src, dst, base in side:
                        from_, to = src.at[:, columns(PLANE + e)], dst.at[1, rows(base, p)]

                        @pl.when(extra == p)
                        def _():
                            pltpu.make_async_copy(from_, to, recv_sem.at[1, group]).start()

                        @pl.when(extra != p)
                        def _():
                            remote(from_, to, send_sem.at[1, n], recv_sem.at[1, group], plane_device(z, extra))

            return carry

        lax.fori_loop(begin, end, step, 0)

    def scatter_first(away, begin=0, end=HEAD):
        @pl.when(lower)
        def _():
            scatter(query_side, x, away, begin, end)

        @pl.when(jnp.logical_not(lower))
        def _():
            scatter(key_side, x, away, begin, end)

    def scatter_rest(away, begin=0, end=HEAD):
        @pl.when(lower)
        def _():
            scatter(key_side, rest, away, begin, end)

        @pl.when(jnp.logical_not(lower))
        def _():
            scatter(query_side, rest, away, begin, end)

    block = SPAN // X
    stats = (
        (0, lse_out, pl.ds(0, 2), pl.ds(X, 2)),
        (1, delta_out, pl.ds(0, PLANE // 2), pl.ds(PLANE, PLANE // 2)),
    )

    def forward_stats(slot):
        await_bytes(lse_out.at[slot, pl.ds(0, X)], stat_recv.at[0, slot])
        await_bytes(delta_out.at[slot, pl.ds(0, PLANE)], stat_recv.at[1, slot])
        for n, ref, near, far in stats:
            remote(ref.at[slot, near], ref.at[slot, far], z_stat.at[0, slot, n], z_stat.at[1, slot, n], down)

    def pieces(xs):
        here = pl.ds(pl.multiple_of(HALO + xs * block, block), block)
        there = pl.ds(pl.multiple_of((xs - X // 2) * block, block), block)
        low_here = pl.ds(pl.multiple_of(xs * block, block), block)
        low_there = pl.ds(pl.multiple_of(SPAN + xs * block, block), block)
        return ((k_out, here, there), (v_out, here, there)), ((q_out, low_here, low_there), (g_out, low_here, low_there))

    def forward(slot, xs):
        await_bytes(k_out.at[slot, pl.ds(0, 2 * block)], recv_sem.at[slot, xs])
        keys, queries = pieces(xs)

        @pl.when(xs >= X // 2)
        def _():
            for n, (ref, here, there) in enumerate(keys):
                remote(ref.at[slot, here], ref.at[slot, there], z_send.at[slot, xs, n], z_recv.at[slot, xs, n], up)

        @pl.when(xs < X // 2)
        def _():
            for n, (ref, here, there) in enumerate(queries):
                remote(ref.at[slot, here], ref.at[slot, there], z_send.at[slot, xs, n], z_recv.at[slot, xs, n], down)

    def finish(slot):
        await_bytes(k_out.at[:, pl.ds(0, 2 * HALO)], recv_sem.at[slot, rest])
        for xs in range(X):
            for n in range(2):
                await_bytes(k_out.at[slot, pl.ds(0, block)], z_send.at[slot, xs, n])
                await_bytes(k_out.at[slot, pl.ds(0, block)], z_recv.at[slot, xs, n])
        for n, ref, near, far in stats:
            await_bytes(ref.at[slot, near], z_stat.at[0, slot, n])
            await_bytes(ref.at[slot, far], z_stat.at[1, slot, n])

    def forward_from(away):
        for d in away:
            xs = (x + X - d) % X
            forward(0, xs)

            @pl.when(owner)
            def _():
                forward(1, xs)

    sides, ends = (1, 3), (2, 0)
    scatter_first(sides)
    for load in loads:
        load.wait()
    local_statistics(p, grad, output, norm, lse_in, delta_in)
    for j in range(5):
        h = head * 5 + j
        slot = h // PLANE
        target = jnp.where(h < PLANE, h, extra_owner(h - PLANE))
        src, dst = lse_in.at[j], lse_out.at[slot, x]

        @pl.when(target == p)
        def _():
            pltpu.make_async_copy(src, dst, stat_recv.at[0, slot]).start()

        @pl.when(target != p)
        def _():
            remote(src, dst, stat_send.at[j], stat_recv.at[0, slot], plane_device(z, target))

    def delta_main(i, carry):
        peer = (p + i) % PLANE
        remote(delta_in.at[peer], delta_out.at[0, p], stat_send.at[5], stat_recv.at[1, 0], plane_device(z, peer))
        return carry

    lax.fori_loop(1, PLANE, delta_main, 0)
    pltpu.make_async_copy(delta_in.at[p], delta_out.at[0, p], stat_recv.at[1, 0]).start()

    def delta_extra(e, carry):
        peer = extra_owner(e)
        src, dst = delta_in.at[PLANE + e], delta_out.at[1, p]

        @pl.when(peer == p)
        def _():
            pltpu.make_async_copy(src, dst, stat_recv.at[1, 1]).start()

        @pl.when(peer != p)
        def _():
            remote(src, dst, stat_send.at[6], stat_recv.at[1, 1], plane_device(z, peer))

        return carry

    lax.fori_loop(0, EXTRA, delta_extra, 0)

    scatter_first(ends)
    prepare(z, lengths, plan_out, start_out)
    forward_from(sides)
    scatter_rest(sides)
    forward_from(ends)
    scatter_rest(ends)

    forward_stats(0)

    @pl.when(owner)
    def _():
        forward_stats(1)

    finish(0)

    @pl.when(owner)
    def _():
        finish(1)

    for j in range(5):
        h = head * 5 + j
        target = jnp.where(h < PLANE, h, extra_owner(h - PLANE))

        @pl.when(target != p)
        def _():
            await_bytes(lse_in.at[j], stat_send.at[j])

    await_bytes(delta_in.at[pl.ds(0, PLANE - 1)], stat_send.at[5])
    for n in range(4):
        await_bytes(k_out.at[0, pl.ds(0, (PLANE - 1) * ROWS)], send_sem.at[0, n])

    @pl.when(owner)
    def _():
        await_bytes(delta_in.at[pl.ds(0, EXTRA - 1)], stat_send.at[6])
        for n in range(4):
            await_bytes(k_out.at[0, pl.ds(0, (EXTRA - 1) * ROWS)], send_sem.at[1, n])

    @pl.when(jnp.logical_not(owner))
    def _():
        await_bytes(delta_in.at[pl.ds(0, EXTRA)], stat_send.at[6])
        for n in range(4):
            await_bytes(k_out.at[0, pl.ds(0, EXTRA * ROWS)], send_sem.at[1, n])


def gather(lengths, q, k, v, g, o, norm):
    wide = pltpu.VMEM((2, WIDE, HD), jnp.bfloat16)
    heads = PLANE + EXTRA
    lengths, q, k, v, g, o, norm = (
        pltpu.with_memory_space_constraint(a, pltpu.HBM) for a in (lengths, q, k, v, g, o, norm)
    )
    return pl.pallas_call(
        gather_kernel,
        name="gather_heads",
        out_shape=(
            wide, wide, wide, wide,
            pltpu.VMEM((2, 6, 4, 128), jnp.float32),
            pltpu.VMEM((2, PLANE + PLANE // 2, 1, 128), jnp.float32),
            pltpu.VMEM((N_TILE, 1, TILE), jnp.int32),
            pltpu.SMEM((2 * N_TILE,), jnp.int32),
        ),
        in_specs=[pl.BlockSpec(memory_space=pltpu.HBM)] * 7,
        out_specs=[pl.BlockSpec(memory_space=pltpu.VMEM)] * 7 + [pl.BlockSpec(memory_space=pltpu.SMEM)],
        scratch_shapes=[
            pltpu.SMEM(lengths.shape, lengths.dtype),
            pltpu.VMEM(g.shape, g.dtype),
            pltpu.VMEM(o.shape, o.dtype),
            pltpu.VMEM(norm.shape, norm.dtype),
            pltpu.VMEM((heads // HEAD, 4, 128), jnp.float32),
            pltpu.VMEM((heads, 1, 128), jnp.float32),
            pltpu.SemaphoreType.DMA((2, 4)),
            pltpu.SemaphoreType.DMA((7,)),
            pltpu.SemaphoreType.DMA((2, X + 1)),
            pltpu.SemaphoreType.DMA((2, X, 2)),
            pltpu.SemaphoreType.DMA((2, X, 2)),
            pltpu.SemaphoreType.DMA((2, 2, 2)),
            pltpu.SemaphoreType.DMA((2, 2)),
            pltpu.SemaphoreType.DMA((4,)),
        ],
        compiler_params=pltpu.CompilerParams(has_side_effects=True, collective_id=0, vmem_limit_bytes=24 * 2**20),
    )(lengths, q, k, v, g, o, norm)


def attention_kernel(
    plan, q_ref, k_ref, v_ref, g_ref, lse_ref, delta_ref, start_t, dq_ref, dk_ref, dv_ref,
    dq_acc, dk_acc, dv_acc, lse_t, delta_t,
):
    scaling = 1.0 / math.sqrt(HD)

    def run(slots):
        for s in slots:
            for i in range(N_TILE):
                lse, delta = [], []
                for c in range(2 * i, 2 * i + 2):
                    lse.append(lse_ref[s, c // 4, pl.ds(c % 4, 1), :] * LOG2E)
                    delta.append(delta_ref[s, 2 * c] + delta_ref[s, 2 * c + 1])
                lse_t[s, i] = jnp.concatenate(lse, axis=1)
                delta_t[s, i] = jnp.concatenate(delta, axis=1)
            dq_acc[s] = jnp.zeros(dq_acc.shape[1:], jnp.float32)

        def key_tile(j, carry):
            key_rows = pl.ds(pl.multiple_of(j * TILE, TILE), TILE)

            begin, end = plan[2 * j], plan[2 * j + 1]

            @pl.when(end <= begin)
            def _():
                for s in slots:
                    dk_ref[s, key_rows] = jnp.zeros((TILE, HD), jnp.bfloat16)
                    dv_ref[s, key_rows] = jnp.zeros((TILE, HD), jnp.bfloat16)

            @pl.when(end > begin)
            def _():
                for s in slots:
                    dk_acc[s] = jnp.zeros((TILE, HD), jnp.float32)
                    dv_acc[s] = jnp.zeros((TILE, HD), jnp.float32)
                key_pos = j * TILE - HALO + lax.broadcasted_iota(jnp.int32, (TILE, 1), 0)
                keys = [k_ref[s, key_rows] for s in slots]
                values = [v_ref[s, key_rows] for s in slots]
                keys_t = [key.T for key in keys]

                def tiles(i, count):
                    query_rows = pl.ds(pl.multiple_of(i * TILE, TILE), TILE * count)

                    def along(read):
                        return jnp.concatenate([read(i + m) for m in range(count)], axis=1)

                    query_pos = i * TILE + lax.broadcasted_iota(jnp.int32, (1, TILE * count), 1)
                    live = (key_pos <= query_pos) & (key_pos >= along(lambda at: start_t[at]))
                    raw = [
                        (
                            lax.dot_general(keys[s], q_ref[s, query_rows], NT, preferred_element_type=jnp.float32),
                            lax.dot_general(values[s], g_ref[s, query_rows], NT, preferred_element_type=jnp.float32),
                        )
                        for s in slots
                    ]
                    low = []
                    for s in slots:
                        score, dweight = raw[s]
                        weight = jnp.exp2(score * (scaling * LOG2E) - along(lambda at: lse_t[s, at]))
                        weight = jnp.where(live, weight, 0.0)
                        dscore = weight * (dweight - along(lambda at: delta_t[s, at]))
                        low.append((weight.astype(jnp.bfloat16), dscore.astype(jnp.bfloat16)))
                    for s in slots:
                        weight, dscore = low[s]
                        dv_acc[s] += jnp.dot(weight, g_ref[s, query_rows], preferred_element_type=jnp.float32)
                        dk_acc[s] += jnp.dot(dscore, q_ref[s, query_rows], preferred_element_type=jnp.float32)
                        for m in range(count):
                            part = dscore[:, m * TILE : (m + 1) * TILE]
                            dq_acc[s, i + m] += jnp.dot(keys_t[s], part, preferred_element_type=jnp.float32)

                def several(t, carry):
                    tiles(begin + AT_ONCE * t, AT_ONCE)
                    return carry

                def single(i, carry):
                    tiles(i, 1)
                    return carry

                groups = (end - begin) // AT_ONCE
                lax.fori_loop(0, groups, several, 0)
                lax.fori_loop(begin + AT_ONCE * groups, end, single, 0)
                for s in slots:
                    dk_ref[s, key_rows] = (dk_acc[s] * scaling).astype(jnp.bfloat16)
                    dv_ref[s, key_rows] = dv_acc[s].astype(jnp.bfloat16)

            return carry

        lax.fori_loop(0, N_TILE, key_tile, 0)
        for s in slots:

            def store(i, carry):
                query_rows = pl.ds(pl.multiple_of(i * TILE, TILE), TILE)
                dq_ref[s, query_rows] = (dq_acc[s, i] * scaling).T.astype(jnp.bfloat16)
                return carry

            lax.fori_loop(0, N_TILE, store, 0)

    z, x, head, _ = place()
    owner, _ = own_extra(x, head)

    @pl.when(owner)
    def _():
        run((0, 1))

    @pl.when(jnp.logical_not(owner))
    def _():
        run((0,))


def attention(plan, q, k, v, g, lse, delta, start):
    shape = pltpu.VMEM((2, WIDE, HD), jnp.bfloat16)
    whole = pl.BlockSpec(memory_space=pltpu.VMEM)
    return pl.pallas_call(
        attention_kernel,
        name="attention_backward",
        out_shape=(shape, shape, shape),
        in_specs=[pl.BlockSpec(memory_space=pltpu.SMEM)] + [whole] * 7,
        out_specs=[whole] * 3,
        scratch_shapes=[
            pltpu.VMEM((2, N_TILE, HD, TILE), jnp.float32),
            pltpu.VMEM((2, TILE, HD), jnp.float32),
            pltpu.VMEM((2, TILE, HD), jnp.float32),
            pltpu.VMEM((2, N_TILE, 1, TILE), jnp.float32),
            pltpu.VMEM((2, N_TILE, 1, TILE), jnp.float32),
        ],
        compiler_params=pltpu.CompilerParams(vmem_limit_bytes=24 * 2**20),
    )(plan, q, k, v, g, lse, delta, start)


def scatter_kernel(
    dq_in, dk_in, dv_in, dq_out, dk_out, dv_out, halo, part, total, send_sem, recv_sem, z_send, z_recv, load_sem
):
    z, x, head, p = place()
    owner, e_own = own_extra(x, head)
    up = {"ctx": ((z + 1) % Z) * X + x, "head": head}
    down = {"ctx": ((z + Z - 1) % Z) * X + x, "head": head}
    barrier = greet(z, x, head, p)
    half = PLANE // 2
    ins, outs, bases = (dq_in, dk_in, dv_in), (dq_out, dk_out, dv_out), (0, HALO, HALO)
    sent = (pl.ds(SPAN, HALO), pl.ds(0, HALO), pl.ds(0, HALO))
    kept = (pl.ds(0, HALO), pl.ds(SPAN, HALO), pl.ds(SPAN, HALO))

    def exchange(slot):
        for n, device in ((1, down), (0, up), (2, down)):
            remote(ins[n].at[slot, sent[n]], halo.at[slot, n], z_send.at[slot, n], z_recv.at[slot, n], device)
        for n in range(3):
            pltpu.make_async_copy(ins[n].at[slot, kept[n]], part.at[slot, n], load_sem.at[slot, n]).start()

    def deliver(slot, at, n, src, peer):
        dst = outs[n].at[:, columns(at)]

        @pl.when(peer == p)
        def _():
            pltpu.make_async_copy(src, dst, recv_sem.at[n]).start()

        @pl.when(peer != p)
        def _():
            remote(src, dst, send_sem.at[slot, n], recv_sem.at[n], plane_device(z, peer))

    def combine(slot, n):
        await_bytes(part.at[slot, n], load_sem.at[slot, n])
        await_bytes(halo.at[slot, n], z_recv.at[slot, n])
        total[slot, n] = (part[slot, n].astype(jnp.float32) + halo[slot, n].astype(jnp.float32)).astype(jnp.bfloat16)

    def phase(*halves):
        def send(slot, at):
            def step(i, carry):
                to_head = (head + turn(i)) % HEAD
                for c in range(2):
                    for n, upper, combined in halves:
                        near = (x + c) % 2 * HEAD + to_head
                        peer = upper * half + near
                        src = total.at[slot, n, rows(0, near)] if combined else ins[n].at[slot, rows(bases[n], peer)]
                        deliver(slot, at, n, src, peer)
                return carry

            lax.fori_loop(0, HEAD, step, 0)

        send(0, p)

        @pl.when(owner)
        def _():
            send(1, PLANE + e_own)

    def combine_all(*arrays):
        for n in arrays:
            combine(0, n)

            @pl.when(owner)
            def _():
                combine(1, n)

    def finish(slot):
        for n in range(3):
            await_bytes(halo.at[slot, n], z_send.at[slot, n])
            await_bytes(ins[n].at[slot, pl.ds(0, (PLANE - 1) * ROWS)], send_sem.at[slot, n])

    pl.semaphore_wait(barrier, PLANE + 1)
    exchange(0)

    @pl.when(owner)
    def _():
        exchange(1)

    phase((0, 1, False), (1, 0, False), (2, 0, False))
    combine_all(1)
    phase((1, 1, True))
    combine_all(0)
    phase((0, 0, True))
    combine_all(2)
    phase((2, 1, True))
    for n in range(3):
        await_bytes(outs[n], recv_sem.at[n])
    finish(0)

    @pl.when(owner)
    def _():
        finish(1)


def scatter(dq, dk, dv):
    shape = jax.ShapeDtypeStruct((ROWS, (PLANE + EXTRA) * HD), jnp.bfloat16)
    buffer = pltpu.VMEM((2, 3, HALO, HD), jnp.bfloat16)
    return pl.pallas_call(
        scatter_kernel,
        name="scatter_heads",
        out_shape=(shape, shape, shape),
        in_specs=[pl.BlockSpec(memory_space=pl.ANY)] * 3,
        out_specs=[pl.BlockSpec(memory_space=pl.ANY)] * 3,
        scratch_shapes=[
            buffer, buffer, buffer,
            pltpu.SemaphoreType.DMA((2, 3)),
            pltpu.SemaphoreType.DMA((3,)),
            pltpu.SemaphoreType.DMA((2, 3)),
            pltpu.SemaphoreType.DMA((2, 3)),
            pltpu.SemaphoreType.DMA((2, 3)),
        ],
        compiler_params=pltpu.CompilerParams(has_side_effects=True, collective_id=1, vmem_limit_bytes=24 * 2**20),
    )(dq, dk, dv)


def on_device(queries, keys, values, outputs, out_grad, log_norms, doc_lengths):
    q, k, v, g, lse, delta, start, plan = gather(
        doc_lengths, queries, keys, values, out_grad, outputs, log_norms.T
    )
    dq, dk, dv = attention(plan, q, k, v, g, lse, delta, start)
    return scatter(dq, dk, dv)


def solution(mesh):
    row = P(("ctx", "head"), None)
    return jax.shard_map(
        on_device,
        mesh=mesh,
        in_specs=(row, row, row, row, row, P("ctx", "head"), P()),
        out_specs=(row, row, row),
        check_vma=False,
    )
```

```python
import math

import jax
import jax.numpy as jnp
from jax import lax
from jax.experimental import pallas as pl
from jax.experimental.pallas import tpu as pltpu
from jax.sharding import PartitionSpec as P

NT = (((1,), (1,)), ((), ()))
MESH = pl.DeviceIdType.MESH
HD = 128
X, HEAD, Z = 4, 8, 8
PLANE = X * HEAD
ROWS = 64
SPAN = PLANE * ROWS
HALO = SPAN // 2
WIDE = SPAN + HALO
EXTRA = 8
TILE = 256
N_TILE = WIDE // TILE
AT_ONCE = 3
DOCS = 16
LOG2E = math.log2(math.e)


def place():
    ctx, head = lax.axis_index("ctx"), lax.axis_index("head")
    z, x = ctx // X, ctx % X
    return z, x, head, x * HEAD + head


def extra_owner(e):
    x = e // 2
    return x * HEAD + (2 * (e % 2) + x % 2) * 2


def own_extra(x, head):
    y, core = head // 2, head % 2
    return (core == 0) & ((x + y) % 2 == 0), x * 2 + y // 2


def shares(x, head):
    return (x + head // 2) % 2 == 0


def plane_device(z, peer):
    return {"ctx": z * X + peer // HEAD, "head": peer % HEAD}


def turn(i):
    return (2 + 4 * (i % 2) + 2 * (i // 2 % 2) + i // 4) % HEAD


def columns(head):
    return pl.ds(pl.multiple_of(head * HD, HD), HD)


def rows(base, peer):
    return pl.ds(pl.multiple_of(base + peer * ROWS, ROWS), ROWS)


def greet(z, x, head, p):
    barrier = pltpu.get_barrier_semaphore()

    for i in range(1, PLANE):
        pl.semaphore_signal(barrier, inc=1, device_id=plane_device(z, (p + i) % PLANE), device_id_type=MESH)
    for step in (1, Z - 1):
        pl.semaphore_signal(barrier, inc=1, device_id={"ctx": ((z + step) % Z) * X + x, "head": head}, device_id_type=MESH)
    return barrier


def remote(src, dst, send, recv, device):
    pltpu.make_async_remote_copy(
        src_ref=src, dst_ref=dst, send_sem=send, recv_sem=recv, device_id=device, device_id_type=MESH
    ).start()


def await_bytes(ref, sem):
    pltpu.make_async_copy(ref, ref, sem).wait()


def local_statistics(p, grad, output, norm, lse, delta):
    heads = delta.shape[0]
    product = grad[...].astype(jnp.float32) * output[...].astype(jnp.float32)
    high = product.astype(jnp.bfloat16)
    low = (product - high.astype(jnp.float32)).astype(jnp.bfloat16)
    head_of = lax.broadcasted_iota(jnp.int32, (heads, heads * HD), 1) // HD
    select = jnp.where(head_of == lax.broadcasted_iota(jnp.int32, (heads, heads * HD), 0), 1.0, 0.0).astype(jnp.bfloat16)
    sums = lax.dot_general(select, high, NT, preferred_element_type=jnp.float32)
    sums += lax.dot_general(select, low, NT, preferred_element_type=jnp.float32)
    empty = jnp.zeros_like(sums)
    wide = jnp.where(p % 2 == 0, jnp.concatenate([sums, empty], axis=1), jnp.concatenate([empty, sums], axis=1))
    for h in range(heads):
        delta[h] = wide[h : h + 1]
    for j in range(lse.shape[0]):
        for c in range(4):
            lse[j, pl.ds(c, 1), :] = norm[pl.ds(j, 1), pl.ds(c * 128, 128)]


def prepare(z, lengths, plan, start_t):
    starts, ends, at = [], [], -z * SPAN
    for d in range(DOCS):
        starts.append(at)
        at = at + lengths[d]
        ends.append(at)
    take_low, take_high = jnp.int32(0), jnp.int32(0)
    for start, end in zip(starts, ends):
        take_low = take_low | ((start < 0) & (end > 0) & (start >= -HALO)).astype(jnp.int32)
        take_high = take_high | ((start < SPAN) & (end > SPAN) & (start < SPAN - HALO)).astype(jnp.int32)
    for j in range(N_TILE):
        first = j * TILE - HALO
        last = first + TILE - 1
        end_last = jnp.int32(1 << 20)
        for end in reversed(ends):
            end_last = jnp.where(end > last, end, end_last)
        limit = jnp.where(take_low > 0, SPAN, 0) if first < 0 else jnp.where(take_high > 0, WIDE, SPAN)
        low = jnp.int32(max(first, 0) // TILE)
        plan[2 * j] = low
        plan[2 * j + 1] = jnp.maximum((jnp.maximum(jnp.minimum(end_last, limit), 0) + TILE - 1) // TILE, low)
    for i in range(N_TILE):
        pos = i * TILE + lax.broadcasted_iota(jnp.int32, (1, TILE), 1)
        own = jnp.full((1, TILE), -(1 << 20), jnp.int32)
        for start in starts:
            own = jnp.where(pos >= start, start, own)
        start_t[i] = own


def gather_kernel(
    lengths_in, q_in, k_in, v_in, g_in, o_in, norm_in,
    q_out, k_out, v_out, g_out, lse_out, delta_out, start_out, plan_out,
    lengths, grad, output, norm, lse_in, delta_in,
    send_sem, stat_send, recv_sem, z_send, z_recv, z_stat, stat_recv, load_sem, mate_send, mate_recv,
):
    z, x, head, p = place()
    owner, e_own = own_extra(x, head)
    barrier = greet(z, x, head, p)
    loads = [
        pltpu.make_async_copy(src, dst, load_sem.at[n])
        for n, (src, dst) in enumerate(((g_in, grad), (o_in, output), (norm_in, norm), (lengths_in, lengths)))
    ]
    for load in loads:
        load.start()
    helper = shares(x, head) & (head % 2 == 1)
    mate = {"ctx": z * X + x, "head": head // 2 * 2 + 1}
    lower = p < PLANE // 2
    up = {"ctx": ((z + 1) % Z) * X + x, "head": head}
    down = {"ctx": ((z + Z - 1) % Z) * X + x, "head": head}
    pl.semaphore_wait(barrier, PLANE + 1)

    query_side = ((0, q_in, q_out, 0), (3, g_in, g_out, 0))
    key_side = ((1, k_in, k_out, HALO), (2, v_in, v_out, HALO))
    rest = X

    def scatter(side, group, away, extra_away):
        def step(i, carry):
            for d in away:
                to_x = (x + d) % X
                peer = to_x * HEAD + (head + turn(i)) % HEAD
                for n, src, dst, base in side:
                    from_, to = src.at[:, columns(peer)], dst.at[0, rows(base, p)]

                    @pl.when(peer == p)
                    def _():
                        pltpu.make_async_copy(from_, to, recv_sem.at[0, group]).start()

                    @pl.when(peer != p)
                    def _():
                        remote(from_, to, send_sem.at[0, n], recv_sem.at[0, group], plane_device(z, peer))

            for d in extra_away:

                @pl.when(i % 4 == 0)
                def _():
                    e = (x + d) % X * 2 + i // 4
                    extra = extra_owner(e)
                    for n, src, dst, base in side:
                        from_, to = src.at[:, columns(PLANE + e)], dst.at[1, rows(base, p)]

                        @pl.when(extra == p)
                        def _():
                            pltpu.make_async_copy(from_, to, recv_sem.at[1, group]).start()

                        @pl.when(extra != p)
                        def _():
                            remote(from_, to, send_sem.at[1, n], recv_sem.at[1, group], plane_device(z, extra))

            return carry

        lax.fori_loop(0, HEAD, step, 0)

    def scatter_first(away, extra_away):
        @pl.when(lower)
        def _():
            scatter(query_side, x, away, extra_away)

        @pl.when(jnp.logical_not(lower))
        def _():
            scatter(key_side, x, away, extra_away)

    def scatter_rest(away, extra_away):
        @pl.when(lower)
        def _():
            scatter(key_side, rest, away, extra_away)

        @pl.when(jnp.logical_not(lower))
        def _():
            scatter(query_side, rest, away, extra_away)

    block = SPAN // X
    stats = (
        (0, lse_out, pl.ds(0, 2), pl.ds(X, 2)),
        (1, delta_out, pl.ds(0, PLANE // 2), pl.ds(PLANE, PLANE // 2)),
    )

    def forward_stats(slot):
        await_bytes(lse_out.at[slot, pl.ds(0, X)], stat_recv.at[0, slot])
        await_bytes(delta_out.at[slot, pl.ds(0, PLANE)], stat_recv.at[1, slot])
        for n, ref, near, far in stats:
            remote(ref.at[slot, near], ref.at[slot, far], z_stat.at[0, slot, n], z_stat.at[1, slot, n], down)

    def pieces(xs):
        here = pl.ds(pl.multiple_of(HALO + xs * block, block), block)
        there = pl.ds(pl.multiple_of((xs - X // 2) * block, block), block)
        low_here = pl.ds(pl.multiple_of(xs * block, block), block)
        low_there = pl.ds(pl.multiple_of(SPAN + xs * block, block), block)
        return ((k_out, here, there), (v_out, here, there)), ((q_out, low_here, low_there), (g_out, low_here, low_there))

    def hand_over(ref, here, kind):
        remote(ref.at[1, here], ref.at[1, here], mate_send.at[kind], mate_recv.at[kind], mate)

    def forward(slot, xs):
        await_bytes(k_out.at[slot, pl.ds(0, 2 * block)], recv_sem.at[slot, xs])
        keys, queries = pieces(xs)
        if slot == 1:

            @pl.when(xs >= X // 2)
            def _():
                for ref, here, there in keys:
                    hand_over(ref, here, 0)

            @pl.when(xs < X // 2)
            def _():
                for ref, here, there in queries:
                    hand_over(ref, here, 1)

        @pl.when(xs >= X // 2)
        def _():
            for n, (ref, here, there) in enumerate(keys):
                remote(ref.at[slot, here], ref.at[slot, there], z_send.at[slot, xs, n], z_recv.at[slot, xs, n], up)

        @pl.when(xs < X // 2)
        def _():
            for n, (ref, here, there) in enumerate(queries):
                remote(ref.at[slot, here], ref.at[slot, there], z_send.at[slot, xs, n], z_recv.at[slot, xs, n], down)

    sides, ends = (1, 3), (2, 0)

    def finish(slot):
        await_bytes(k_out.at[:, pl.ds(0, 2 * HALO)], recv_sem.at[slot, rest])
        if slot == 1:
            for ref in (k_out, v_out):
                hand_over(ref, pl.ds(HALO, HALO), 0)
            for ref in (q_out, g_out):
                hand_over(ref, pl.ds(HALO, HALO), 1)
        for d in sides + ends:
            xs = (x + X - d) % X
            for n in range(2):
                await_bytes(k_out.at[slot, pl.ds(0, block)], z_recv.at[slot, xs, n])
                await_bytes(k_out.at[slot, pl.ds(0, block)], z_send.at[slot, xs, n])
            if slot == 1:
                keys, queries = pieces(xs)

                @pl.when(xs >= X // 2)
                def _():
                    for ref, here, there in keys:
                        hand_over(ref, there, 0)

                @pl.when(xs < X // 2)
                def _():
                    for ref, here, there in queries:
                        hand_over(ref, there, 1)

        for n, ref, near, far in stats:
            await_bytes(ref.at[slot, near], z_stat.at[0, slot, n])
            await_bytes(ref.at[slot, far], z_stat.at[1, slot, n])
        if slot == 1:
            hand_over(lse_out, pl.ds(0, X + 2), 2)
            hand_over(delta_out, pl.ds(0, PLANE + PLANE // 2), 3)

    def handed_over(sems):
        await_bytes(k_out, sems.at[0])
        await_bytes(q_out, sems.at[1])
        await_bytes(lse_out.at[1], sems.at[2])
        await_bytes(delta_out.at[1], sems.at[3])

    def forward_from(away):
        for d in away:
            xs = (x + X - d) % X

            @pl.when(owner)
            def _():
                forward(1, xs)

            forward(0, xs)

    scatter_first(sides, sides)
    scatter_first(ends, ends)
    for load in loads:
        load.wait()
    local_statistics(p, grad, output, norm, lse_in, delta_in)
    forward_from(sides)
    for j in range(5):
        h = head * 5 + j
        slot = h // PLANE
        target = jnp.where(h < PLANE, h, extra_owner(h - PLANE))
        src, dst = lse_in.at[j], lse_out.at[slot, x]

        @pl.when(target == p)
        def _():
            pltpu.make_async_copy(src, dst, stat_recv.at[0, slot]).start()

        @pl.when(target != p)
        def _():
            remote(src, dst, stat_send.at[j], stat_recv.at[0, slot], plane_device(z, target))

    def delta_main(i, carry):
        peer = (p + i) % PLANE
        remote(delta_in.at[peer], delta_out.at[0, p], stat_send.at[5], stat_recv.at[1, 0], plane_device(z, peer))
        return carry

    lax.fori_loop(1, PLANE, delta_main, 0)
    pltpu.make_async_copy(delta_in.at[p], delta_out.at[0, p], stat_recv.at[1, 0]).start()

    def delta_extra(e, carry):
        peer = extra_owner(e)
        src, dst = delta_in.at[PLANE + e], delta_out.at[1, p]

        @pl.when(peer == p)
        def _():
            pltpu.make_async_copy(src, dst, stat_recv.at[1, 1]).start()

        @pl.when(peer != p)
        def _():
            remote(src, dst, stat_send.at[6], stat_recv.at[1, 1], plane_device(z, peer))

        return carry

    lax.fori_loop(0, EXTRA, delta_extra, 0)

    scatter_rest(sides, sides + ends)
    forward_from(ends)
    scatter_rest(ends, ())
    prepare(z, lengths, plan_out, start_out)
    forward_stats(0)

    @pl.when(owner)
    def _():
        forward_stats(1)

    @pl.when(owner)
    def _():
        finish(1)

    finish(0)

    @pl.when(owner)
    def _():
        handed_over(mate_send)

    @pl.when(helper)
    def _():
        handed_over(mate_recv)

    for j in range(5):
        h = head * 5 + j
        target = jnp.where(h < PLANE, h, extra_owner(h - PLANE))

        @pl.when(target != p)
        def _():
            await_bytes(lse_in.at[j], stat_send.at[j])

    await_bytes(delta_in.at[pl.ds(0, PLANE - 1)], stat_send.at[5])
    for n in range(4):
        await_bytes(k_out.at[0, pl.ds(0, (PLANE - 1) * ROWS)], send_sem.at[0, n])

    @pl.when(owner)
    def _():
        await_bytes(delta_in.at[pl.ds(0, EXTRA - 1)], stat_send.at[6])
        for n in range(4):
            await_bytes(k_out.at[0, pl.ds(0, (EXTRA - 1) * ROWS)], send_sem.at[1, n])

    @pl.when(jnp.logical_not(owner))
    def _():
        await_bytes(delta_in.at[pl.ds(0, EXTRA)], stat_send.at[6])
        for n in range(4):
            await_bytes(k_out.at[0, pl.ds(0, EXTRA * ROWS)], send_sem.at[1, n])


def gather(lengths, q, k, v, g, o, norm):
    wide = pltpu.VMEM((2, WIDE, HD), jnp.bfloat16)
    heads = PLANE + EXTRA
    lengths, q, k, v, g, o, norm = (
        pltpu.with_memory_space_constraint(a, pltpu.HBM) for a in (lengths, q, k, v, g, o, norm)
    )
    return pl.pallas_call(
        gather_kernel,
        name="gather_heads",
        out_shape=(
            wide, wide, wide, wide,
            pltpu.VMEM((2, 6, 4, 128), jnp.float32),
            pltpu.VMEM((2, PLANE + PLANE // 2, 1, 128), jnp.float32),
            pltpu.VMEM((N_TILE, 1, TILE), jnp.int32),
            pltpu.SMEM((2 * N_TILE,), jnp.int32),
        ),
        in_specs=[pl.BlockSpec(memory_space=pltpu.HBM)] * 7,
        out_specs=[pl.BlockSpec(memory_space=pltpu.VMEM)] * 7 + [pl.BlockSpec(memory_space=pltpu.SMEM)],
        scratch_shapes=[
            pltpu.SMEM(lengths.shape, lengths.dtype),
            pltpu.VMEM(g.shape, g.dtype),
            pltpu.VMEM(o.shape, o.dtype),
            pltpu.VMEM(norm.shape, norm.dtype),
            pltpu.VMEM((heads // HEAD, 4, 128), jnp.float32),
            pltpu.VMEM((heads, 1, 128), jnp.float32),
            pltpu.SemaphoreType.DMA((2, 4)),
            pltpu.SemaphoreType.DMA((7,)),
            pltpu.SemaphoreType.DMA((2, X + 1)),
            pltpu.SemaphoreType.DMA((2, X, 2)),
            pltpu.SemaphoreType.DMA((2, X, 2)),
            pltpu.SemaphoreType.DMA((2, 2, 2)),
            pltpu.SemaphoreType.DMA((2, 2)),
            pltpu.SemaphoreType.DMA((4,)),
            pltpu.SemaphoreType.DMA((4,)),
            pltpu.SemaphoreType.DMA((4,)),
        ],
        compiler_params=pltpu.CompilerParams(has_side_effects=True, collective_id=0, vmem_limit_bytes=24 * 2**20),
    )(lengths, q, k, v, g, o, norm)


def attention_kernel(
    plan, q_ref, k_ref, v_ref, g_ref, lse_ref, delta_ref, start_t, dq_ref, dk_ref, dv_ref,
    dq_acc, dk_acc, dv_acc, lse_t, delta_t,
):
    scaling = 1.0 / math.sqrt(HD)

    z, x, head, _ = place()
    shared = shares(x, head)

    def begin_slot(s):
        for i in range(N_TILE):
            lse, delta = [], []
            for c in range(2 * i, 2 * i + 2):
                lse.append(lse_ref[s, c // 4, pl.ds(c % 4, 1), :] * LOG2E)
                delta.append(delta_ref[s, 2 * c] + delta_ref[s, 2 * c + 1])
            lse_t[s, i] = jnp.concatenate(lse, axis=1)
            delta_t[s, i] = jnp.concatenate(delta, axis=1)
        dq_acc[s] = jnp.zeros(dq_acc.shape[1:], jnp.float32)

    def end_slot(s):
        def store(i, carry):
            query_rows = pl.ds(pl.multiple_of(i * TILE, TILE), TILE)
            dq_ref[s, query_rows] = (dq_acc[s, i] * scaling).T.astype(jnp.bfloat16)
            return carry

        lax.fori_loop(0, N_TILE, store, 0)

    def key_tile(j, carry):
        key_rows = pl.ds(pl.multiple_of(j * TILE, TILE), TILE)

        begin, end = plan[2 * j], plan[2 * j + 1]

        both = shared & (j % 2 == head % 2)
        alive = end > begin

        def skip(s):
            dk_ref[s, key_rows] = jnp.zeros((TILE, HD), jnp.bfloat16)
            dv_ref[s, key_rows] = jnp.zeros((TILE, HD), jnp.bfloat16)

        def work(slots):
            for s in slots:
                dk_acc[s] = jnp.zeros((TILE, HD), jnp.float32)
                dv_acc[s] = jnp.zeros((TILE, HD), jnp.float32)
            key_pos = j * TILE - HALO + lax.broadcasted_iota(jnp.int32, (TILE, 1), 0)
            keys = [k_ref[s, key_rows] for s in slots]
            values = [v_ref[s, key_rows] for s in slots]
            keys_t = [key.T for key in keys]

            def tiles(i, count):
                query_rows = pl.ds(pl.multiple_of(i * TILE, TILE), TILE * count)

                def along(read):
                    return jnp.concatenate([read(i + m) for m in range(count)], axis=1)

                query_pos = i * TILE + lax.broadcasted_iota(jnp.int32, (1, TILE * count), 1)
                live = (key_pos <= query_pos) & (key_pos >= along(lambda at: start_t[at]))
                raw = [
                    (
                        lax.dot_general(keys[s], q_ref[s, query_rows], NT, preferred_element_type=jnp.float32),
                        lax.dot_general(values[s], g_ref[s, query_rows], NT, preferred_element_type=jnp.float32),
                    )
                    for s in slots
                ]
                low = []
                for s in slots:
                    score, dweight = raw[s]
                    weight = jnp.exp2(score * (scaling * LOG2E) - along(lambda at: lse_t[s, at]))
                    weight = jnp.where(live, weight, 0.0)
                    dscore = weight * (dweight - along(lambda at: delta_t[s, at]))
                    low.append((weight.astype(jnp.bfloat16), dscore.astype(jnp.bfloat16)))
                for s in slots:
                    weight, dscore = low[s]
                    dv_acc[s] += jnp.dot(weight, g_ref[s, query_rows], preferred_element_type=jnp.float32)
                    dk_acc[s] += jnp.dot(dscore, q_ref[s, query_rows], preferred_element_type=jnp.float32)
                    for m in range(count):
                        part = dscore[:, m * TILE : (m + 1) * TILE]
                        dq_acc[s, i + m] += jnp.dot(keys_t[s], part, preferred_element_type=jnp.float32)

            def several(t, carry):
                tiles(begin + AT_ONCE * t, AT_ONCE)
                return carry

            def single(i, carry):
                tiles(i, 1)
                return carry

            groups = (end - begin) // AT_ONCE
            lax.fori_loop(0, groups, several, 0)
            lax.fori_loop(begin + AT_ONCE * groups, end, single, 0)
            for s in slots:
                dk_ref[s, key_rows] = (dk_acc[s] * scaling).astype(jnp.bfloat16)
                dv_ref[s, key_rows] = dv_acc[s].astype(jnp.bfloat16)

        @pl.when(alive & both)
        def _():
            work((0, 1))

        @pl.when(alive & jnp.logical_not(both))
        def _():
            work((0,))

        @pl.when(jnp.logical_not(alive))
        def _():
            skip(0)

        @pl.when(shared & jnp.logical_not(alive & both))
        def _():
            skip(1)

        return carry

    begin_slot(0)

    @pl.when(shared)
    def _():
        begin_slot(1)

    lax.fori_loop(0, N_TILE, key_tile, 0)
    end_slot(0)

    @pl.when(shared)
    def _():
        end_slot(1)


def attention(plan, q, k, v, g, lse, delta, start):
    shape = pltpu.VMEM((2, WIDE, HD), jnp.bfloat16)
    whole = pl.BlockSpec(memory_space=pltpu.VMEM)
    return pl.pallas_call(
        attention_kernel,
        name="attention_backward",
        out_shape=(shape, shape, shape),
        in_specs=[pl.BlockSpec(memory_space=pltpu.SMEM)] + [whole] * 7,
        out_specs=[whole] * 3,
        scratch_shapes=[
            pltpu.VMEM((2, N_TILE, HD, TILE), jnp.float32),
            pltpu.VMEM((2, TILE, HD), jnp.float32),
            pltpu.VMEM((2, TILE, HD), jnp.float32),
            pltpu.VMEM((2, N_TILE, 1, TILE), jnp.float32),
            pltpu.VMEM((2, N_TILE, 1, TILE), jnp.float32),
        ],
        compiler_params=pltpu.CompilerParams(vmem_limit_bytes=24 * 2**20),
    )(plan, q, k, v, g, lse, delta, start)


def scatter_kernel(
    dq_in, dk_in, dv_in, dq_out, dk_out, dv_out,
    halo, part, total, theirs, joined, send_sem, recv_sem, z_send, z_recv, load_sem, mate_send, mate_recv,
):
    z, x, head, p = place()
    owner, e_own = own_extra(x, head)
    up = {"ctx": ((z + 1) % Z) * X + x, "head": head}
    down = {"ctx": ((z + Z - 1) % Z) * X + x, "head": head}
    barrier = greet(z, x, head, p)
    half = PLANE // 2
    ins, outs, bases = (dq_in, dk_in, dv_in), (dq_out, dk_out, dv_out), (0, HALO, HALO)
    sent = (pl.ds(SPAN, HALO), pl.ds(0, HALO), pl.ds(0, HALO))
    kept = (pl.ds(0, HALO), pl.ds(SPAN, HALO), pl.ds(SPAN, HALO))

    helper = shares(x, head) & (head % 2 == 1)
    mate = {"ctx": z * X + x, "head": head // 2 * 2}

    def own(slot, n, at):
        return ins[n].at[0, at] if slot == 0 else joined.at[n, at]

    def join(n):
        await_bytes(theirs.at[n], mate_recv.at[n])

        def step(i, carry):
            at = pl.ds(pl.multiple_of(i * TILE, TILE), TILE)
            joined[n, at] = (ins[n][1, at].astype(jnp.float32) + theirs[n, at].astype(jnp.float32)).astype(jnp.bfloat16)
            return carry

        lax.fori_loop(0, N_TILE, step, 0)

    def exchange(slot):
        for n, device in ((1, down), (0, up), (2, down)):
            remote(own(slot, n, sent[n]), halo.at[slot, n], z_send.at[slot, n], z_recv.at[slot, n], device)
        for n in range(3):
            pltpu.make_async_copy(own(slot, n, kept[n]), part.at[slot, n], load_sem.at[slot, n]).start()

    def deliver(slot, at, n, src, peer):
        dst = outs[n].at[:, columns(at)]

        @pl.when(peer == p)
        def _():
            pltpu.make_async_copy(src, dst, recv_sem.at[n]).start()

        @pl.when(peer != p)
        def _():
            remote(src, dst, send_sem.at[slot, n], recv_sem.at[n], plane_device(z, peer))

    def combine(slot, n):
        await_bytes(part.at[slot, n], load_sem.at[slot, n])
        await_bytes(halo.at[slot, n], z_recv.at[slot, n])
        total[slot, n] = (part[slot, n].astype(jnp.float32) + halo[slot, n].astype(jnp.float32)).astype(jnp.bfloat16)

    def phase(slot, *halves):
        def send(slot, at):
            def step(i, carry):
                to_head = (head + turn(i)) % HEAD
                for c in range(2):
                    for n, upper, combined in halves:
                        near = (x + c) % 2 * HEAD + to_head
                        peer = upper * half + near
                        src = total.at[slot, n, rows(0, near)] if combined else own(slot, n, rows(bases[n], peer))
                        deliver(slot, at, n, src, peer)
                return carry

            lax.fori_loop(0, HEAD, step, 0)

        send(slot, p if slot == 0 else PLANE + e_own)

    def finish(slot):
        for n in range(3):
            await_bytes(halo.at[slot, n], z_send.at[slot, n])
            await_bytes(ins[n].at[slot, pl.ds(0, (PLANE - 1) * ROWS)], send_sem.at[slot, n])

    pl.semaphore_wait(barrier, PLANE + 1)
    @pl.when(helper)
    def _():
        for n in (1, 0, 2):
            remote(ins[n].at[1], theirs.at[n], mate_send.at[n], mate_recv.at[n], mate)

    early = (0, 1, False), (1, 0, False), (2, 0, False)
    exchange(0)
    phase(0, *early)

    @pl.when(owner)
    def _():
        for n in (1, 0, 2):
            join(n)
        exchange(1)
        phase(1, *early)

    for n, upper in ((1, 1), (0, 0), (2, 1)):
        combine(0, n)
        phase(0, (n, upper, True))

        @pl.when(owner)
        def _():
            combine(1, n)
            phase(1, (n, upper, True))

    @pl.when(helper)
    def _():
        for n in range(3):
            await_bytes(ins[n].at[1], mate_send.at[n])

    for n in range(3):
        await_bytes(outs[n], recv_sem.at[n])
    finish(0)

    @pl.when(owner)
    def _():
        finish(1)


def scatter(dq, dk, dv):
    shape = jax.ShapeDtypeStruct((ROWS, (PLANE + EXTRA) * HD), jnp.bfloat16)
    buffer = pltpu.VMEM((2, 3, HALO, HD), jnp.bfloat16)
    return pl.pallas_call(
        scatter_kernel,
        name="scatter_heads",
        out_shape=(shape, shape, shape),
        in_specs=[pl.BlockSpec(memory_space=pltpu.VMEM)] * 3,
        out_specs=[pl.BlockSpec(memory_space=pl.ANY)] * 3,
        scratch_shapes=[
            buffer, buffer, buffer,
            pltpu.VMEM((3, WIDE, HD), jnp.bfloat16),
            pltpu.VMEM((3, WIDE, HD), jnp.bfloat16),
            pltpu.SemaphoreType.DMA((2, 3)),
            pltpu.SemaphoreType.DMA((3,)),
            pltpu.SemaphoreType.DMA((2, 3)),
            pltpu.SemaphoreType.DMA((2, 3)),
            pltpu.SemaphoreType.DMA((2, 3)),
            pltpu.SemaphoreType.DMA((3,)),
            pltpu.SemaphoreType.DMA((3,)),
        ],
        compiler_params=pltpu.CompilerParams(has_side_effects=True, collective_id=1, vmem_limit_bytes=24 * 2**20),
    )(dq, dk, dv)


def on_device(queries, keys, values, outputs, out_grad, log_norms, doc_lengths):
    q, k, v, g, lse, delta, start, plan = gather(
        doc_lengths, queries, keys, values, out_grad, outputs, log_norms.T
    )
    dq, dk, dv = attention(plan, q, k, v, g, lse, delta, start)
    return scatter(dq, dk, dv)


def solution(mesh):
    row = P(("ctx", "head"), None)
    return jax.shard_map(
        on_device,
        mesh=mesh,
        in_specs=(row, row, row, row, row, P("ctx", "head"), P()),
        out_specs=(row, row, row),
        check_vma=False,
    )
```

```python
import math

import jax
import jax.numpy as jnp
from jax import lax
from jax.experimental import pallas as pl
from jax.experimental.pallas import tpu as pltpu
from jax.sharding import PartitionSpec as P

NT = (((1,), (1,)), ((), ()))
MESH = pl.DeviceIdType.MESH
HD = 128
X, HEAD, Z = 4, 8, 8
PLANE = X * HEAD
ROWS = 64
SPAN = PLANE * ROWS
HALO = SPAN // 2
WIDE = SPAN + HALO
EXTRA = 8
TILE = 256
N_TILE = WIDE // TILE
AT_ONCE = 3
DOCS = 16
LOG2E = math.log2(math.e)


def place():
    ctx, head = lax.axis_index("ctx"), lax.axis_index("head")
    z, x = ctx // X, ctx % X
    return z, x, head, x * HEAD + head


def extra_owner(e):
    x = e // 2
    return x * HEAD + (2 * (e % 2) + x % 2) * 2


def own_extra(x, head):
    y, core = head // 2, head % 2
    return (core == 0) & ((x + y) % 2 == 0), x * 2 + y // 2


def shares(x, head):
    return (x + head // 2) % 2 == 0


def plane_device(z, peer):
    return {"ctx": z * X + peer // HEAD, "head": peer % HEAD}


def turn(i):
    return (2 + 4 * (i % 2) + 2 * (i // 2 % 2) + i // 4) % HEAD


def columns(head):
    return pl.ds(pl.multiple_of(head * HD, HD), HD)


def rows(base, peer):
    return pl.ds(pl.multiple_of(base + peer * ROWS, ROWS), ROWS)


def greet(z, x, head, p):
    barrier = pltpu.get_barrier_semaphore()

    for i in range(1, PLANE):
        pl.semaphore_signal(barrier, inc=1, device_id=plane_device(z, (p + i) % PLANE), device_id_type=MESH)
    for step in (1, Z - 1):
        pl.semaphore_signal(barrier, inc=1, device_id={"ctx": ((z + step) % Z) * X + x, "head": head}, device_id_type=MESH)
    return barrier


def remote(src, dst, send, recv, device):
    pltpu.make_async_remote_copy(
        src_ref=src, dst_ref=dst, send_sem=send, recv_sem=recv, device_id=device, device_id_type=MESH
    ).start()


def await_bytes(ref, sem):
    pltpu.make_async_copy(ref, ref, sem).wait()


def local_statistics(p, grad, output, norm, lse, delta):
    heads = delta.shape[0]
    product = grad[...].astype(jnp.float32) * output[...].astype(jnp.float32)
    high = product.astype(jnp.bfloat16)
    low = (product - high.astype(jnp.float32)).astype(jnp.bfloat16)
    head_of = lax.broadcasted_iota(jnp.int32, (heads, heads * HD), 1) // HD
    select = jnp.where(head_of == lax.broadcasted_iota(jnp.int32, (heads, heads * HD), 0), 1.0, 0.0).astype(jnp.bfloat16)
    sums = lax.dot_general(select, high, NT, preferred_element_type=jnp.float32)
    sums += lax.dot_general(select, low, NT, preferred_element_type=jnp.float32)
    empty = jnp.zeros_like(sums)
    wide = jnp.where(p % 2 == 0, jnp.concatenate([sums, empty], axis=1), jnp.concatenate([empty, sums], axis=1))
    for h in range(heads):
        delta[h] = wide[h : h + 1]
    for j in range(lse.shape[0]):
        for c in range(4):
            lse[j, pl.ds(c, 1), :] = norm[pl.ds(j, 1), pl.ds(c * 128, 128)]


def prepare(z, lengths, plan, start_t):
    starts, ends, at = [], [], -z * SPAN
    for d in range(DOCS):
        starts.append(at)
        at = at + lengths[d]
        ends.append(at)
    take_low, take_high = jnp.int32(0), jnp.int32(0)
    for start, end in zip(starts, ends):
        take_low = take_low | ((start < 0) & (end > 0) & (start >= -HALO)).astype(jnp.int32)
        take_high = take_high | ((start < SPAN) & (end > SPAN) & (start < SPAN - HALO)).astype(jnp.int32)
    for j in range(N_TILE):
        first = j * TILE - HALO
        last = first + TILE - 1
        end_last = jnp.int32(1 << 20)
        for end in reversed(ends):
            end_last = jnp.where(end > last, end, end_last)
        limit = jnp.where(take_low > 0, SPAN, 0) if first < 0 else jnp.where(take_high > 0, WIDE, SPAN)
        low = jnp.int32(max(first, 0) // TILE)
        plan[2 * j] = low
        plan[2 * j + 1] = jnp.maximum((jnp.maximum(jnp.minimum(end_last, limit), 0) + TILE - 1) // TILE, low)
    for i in range(N_TILE):
        pos = i * TILE + lax.broadcasted_iota(jnp.int32, (1, TILE), 1)
        own = jnp.full((1, TILE), -(1 << 20), jnp.int32)
        for start in starts:
            own = jnp.where(pos >= start, start, own)
        start_t[i] = own


def gather_kernel(
    lengths_in, q_in, k_in, v_in, g_in, o_in, norm_in,
    q_out, k_out, v_out, g_out, lse_out, delta_out, start_out, plan_out,
    lengths, grad, output, norm, lse_in, delta_in,
    send_sem, stat_send, recv_sem, z_send, z_recv, z_stat, stat_recv, load_sem, mate_send, mate_recv,
):
    z, x, head, p = place()
    owner, e_own = own_extra(x, head)
    barrier = greet(z, x, head, p)
    loads = [
        pltpu.make_async_copy(src, dst, load_sem.at[n])
        for n, (src, dst) in enumerate(((g_in, grad), (o_in, output), (norm_in, norm), (lengths_in, lengths)))
    ]
    for load in loads:
        load.start()
    helper = shares(x, head) & (head % 2 == 1)
    mate = {"ctx": z * X + x, "head": head // 2 * 2 + 1}
    lower = p < PLANE // 2
    up = {"ctx": ((z + 1) % Z) * X + x, "head": head}
    down = {"ctx": ((z + Z - 1) % Z) * X + x, "head": head}
    pl.semaphore_wait(barrier, PLANE + 1)

    query_side = ((0, q_in, q_out, 0), (3, g_in, g_out, 0))
    key_side = ((1, k_in, k_out, HALO), (2, v_in, v_out, HALO))
    rest = X

    def scatter(side, group, away, extra_away, begin, end):
        def step(i, carry):
            for d in away:
                to_x = (x + d) % X
                peer = to_x * HEAD + (head + turn((i + 2 * d) % HEAD)) % HEAD
                for n, src, dst, base in side:
                    from_, to = src.at[:, columns(peer)], dst.at[0, rows(base, p)]

                    @pl.when(peer == p)
                    def _():
                        pltpu.make_async_copy(from_, to, recv_sem.at[0, group]).start()

                    @pl.when(peer != p)
                    def _():
                        remote(from_, to, send_sem.at[0, n], recv_sem.at[0, group], plane_device(z, peer))

            for d in extra_away:

                @pl.when((i % 2 == 0) & (i < 4))
                def _():
                    e = (x + d) % X * 2 + i // 2
                    extra = extra_owner(e)
                    for n, src, dst, base in side:
                        from_, to = src.at[:, columns(PLANE + e)], dst.at[1, rows(base, p)]

                        @pl.when(extra == p)
                        def _():
                            pltpu.make_async_copy(from_, to, recv_sem.at[1, group]).start()

                        @pl.when(extra != p)
                        def _():
                            remote(from_, to, send_sem.at[1, n], recv_sem.at[1, group], plane_device(z, extra))

            return carry

        lax.fori_loop(begin, end, step, 0)

    def scatter_first(away, extra_away, begin=0, end=HEAD):
        @pl.when(lower)
        def _():
            scatter(query_side, x, away, extra_away, begin, end)

        @pl.when(jnp.logical_not(lower))
        def _():
            scatter(key_side, x, away, extra_away, begin, end)

    def scatter_rest(away, extra_away, begin=0, end=HEAD):
        @pl.when(lower)
        def _():
            scatter(key_side, rest, away, extra_away, begin, end)

        @pl.when(jnp.logical_not(lower))
        def _():
            scatter(query_side, rest, away, extra_away, begin, end)

    block = SPAN // X
    stats = (
        (0, lse_out, pl.ds(0, 2), pl.ds(X, 2)),
        (1, delta_out, pl.ds(0, PLANE // 2), pl.ds(PLANE, PLANE // 2)),
    )

    def forward_stats(slot):
        await_bytes(lse_out.at[slot, pl.ds(0, X)], stat_recv.at[0, slot])
        await_bytes(delta_out.at[slot, pl.ds(0, PLANE)], stat_recv.at[1, slot])
        for n, ref, near, far in stats:
            remote(ref.at[slot, near], ref.at[slot, far], z_stat.at[0, slot, n], z_stat.at[1, slot, n], down)

    def pieces(xs):
        here = pl.ds(pl.multiple_of(HALO + xs * block, block), block)
        there = pl.ds(pl.multiple_of((xs - X // 2) * block, block), block)
        low_here = pl.ds(pl.multiple_of(xs * block, block), block)
        low_there = pl.ds(pl.multiple_of(SPAN + xs * block, block), block)
        return ((k_out, here, there), (v_out, here, there)), ((q_out, low_here, low_there), (g_out, low_here, low_there))

    def hand_over(ref, here, kind):
        remote(ref.at[1, here], ref.at[1, here], mate_send.at[kind], mate_recv.at[kind], mate)

    def forward(slot, xs):
        await_bytes(k_out.at[slot, pl.ds(0, 2 * block)], recv_sem.at[slot, xs])
        keys, queries = pieces(xs)
        if slot == 1:

            @pl.when(xs >= X // 2)
            def _():
                for ref, here, there in keys:
                    hand_over(ref, here, 0)

            @pl.when(xs < X // 2)
            def _():
                for ref, here, there in queries:
                    hand_over(ref, here, 1)

        @pl.when(xs >= X // 2)
        def _():
            for n, (ref, here, there) in enumerate(keys):
                remote(ref.at[slot, here], ref.at[slot, there], z_send.at[slot, xs, n], z_recv.at[slot, xs, n], up)

        @pl.when(xs < X // 2)
        def _():
            for n, (ref, here, there) in enumerate(queries):
                remote(ref.at[slot, here], ref.at[slot, there], z_send.at[slot, xs, n], z_recv.at[slot, xs, n], down)

    sides, ends = (1, 3), (2, 0)

    def finish(slot):
        await_bytes(k_out.at[:, pl.ds(0, 2 * HALO)], recv_sem.at[slot, rest])
        if slot == 1:
            for ref in (k_out, v_out):
                hand_over(ref, pl.ds(HALO, HALO), 0)
            for ref in (q_out, g_out):
                hand_over(ref, pl.ds(HALO, HALO), 1)
        for d in sides + ends:
            xs = (x + X - d) % X
            for n in range(2):
                await_bytes(k_out.at[slot, pl.ds(0, block)], z_recv.at[slot, xs, n])
                await_bytes(k_out.at[slot, pl.ds(0, block)], z_send.at[slot, xs, n])
            if slot == 1:
                keys, queries = pieces(xs)

                @pl.when(xs >= X // 2)
                def _():
                    for ref, here, there in keys:
                        hand_over(ref, there, 0)

                @pl.when(xs < X // 2)
                def _():
                    for ref, here, there in queries:
                        hand_over(ref, there, 1)

        for n, ref, near, far in stats:
            await_bytes(ref.at[slot, near], z_stat.at[0, slot, n])
            await_bytes(ref.at[slot, far], z_stat.at[1, slot, n])
        if slot == 1:
            hand_over(lse_out, pl.ds(0, X + 2), 2)
            hand_over(delta_out, pl.ds(0, PLANE + PLANE // 2), 3)

    def handed_over(sems):
        await_bytes(k_out, sems.at[0])
        await_bytes(q_out, sems.at[1])
        await_bytes(lse_out.at[1], sems.at[2])
        await_bytes(delta_out.at[1], sems.at[3])

    def forward_from(away):
        for d in away:
            xs = (x + X - d) % X

            @pl.when(owner)
            def _():
                forward(1, xs)

            forward(0, xs)

    scatter_first(sides + ends, sides + ends)
    for load in loads:
        load.wait()
    local_statistics(p, grad, output, norm, lse_in, delta_in)
    forward_from(sides)
    for j in range(5):
        h = head * 5 + j
        slot = h // PLANE
        target = jnp.where(h < PLANE, h, extra_owner(h - PLANE))
        src, dst = lse_in.at[j], lse_out.at[slot, x]

        @pl.when(target == p)
        def _():
            pltpu.make_async_copy(src, dst, stat_recv.at[0, slot]).start()

        @pl.when(target != p)
        def _():
            remote(src, dst, stat_send.at[j], stat_recv.at[0, slot], plane_device(z, target))

    def delta_main(i, carry):
        peer = (p + i) % PLANE
        remote(delta_in.at[peer], delta_out.at[0, p], stat_send.at[5], stat_recv.at[1, 0], plane_device(z, peer))
        return carry

    lax.fori_loop(1, PLANE, delta_main, 0)
    pltpu.make_async_copy(delta_in.at[p], delta_out.at[0, p], stat_recv.at[1, 0]).start()

    def delta_extra(e, carry):
        peer = extra_owner(e)
        src, dst = delta_in.at[PLANE + e], delta_out.at[1, p]

        @pl.when(peer == p)
        def _():
            pltpu.make_async_copy(src, dst, stat_recv.at[1, 1]).start()

        @pl.when(peer != p)
        def _():
            remote(src, dst, stat_send.at[6], stat_recv.at[1, 1], plane_device(z, peer))

        return carry

    lax.fori_loop(0, EXTRA, delta_extra, 0)

    scatter_rest(sides + ends, sides + ends, 0, HEAD // 2)
    forward_from(ends)
    scatter_rest(sides + ends, (), HEAD // 2, HEAD)
    prepare(z, lengths, plan_out, start_out)
    forward_stats(0)

    @pl.when(owner)
    def _():
        forward_stats(1)

    @pl.when(owner)
    def _():
        finish(1)

    finish(0)

    @pl.when(owner)
    def _():
        handed_over(mate_send)

    @pl.when(helper)
    def _():
        handed_over(mate_recv)

    for j in range(5):
        h = head * 5 + j
        target = jnp.where(h < PLANE, h, extra_owner(h - PLANE))

        @pl.when(target != p)
        def _():
            await_bytes(lse_in.at[j], stat_send.at[j])

    await_bytes(delta_in.at[pl.ds(0, PLANE - 1)], stat_send.at[5])
    for n in range(4):
        await_bytes(k_out.at[0, pl.ds(0, (PLANE - 1) * ROWS)], send_sem.at[0, n])

    @pl.when(owner)
    def _():
        await_bytes(delta_in.at[pl.ds(0, EXTRA - 1)], stat_send.at[6])
        for n in range(4):
            await_bytes(k_out.at[0, pl.ds(0, (EXTRA - 1) * ROWS)], send_sem.at[1, n])

    @pl.when(jnp.logical_not(owner))
    def _():
        await_bytes(delta_in.at[pl.ds(0, EXTRA)], stat_send.at[6])
        for n in range(4):
            await_bytes(k_out.at[0, pl.ds(0, EXTRA * ROWS)], send_sem.at[1, n])


def gather(lengths, q, k, v, g, o, norm):
    wide = pltpu.VMEM((2, WIDE, HD), jnp.bfloat16)
    heads = PLANE + EXTRA
    lengths, q, k, v, g, o, norm = (
        pltpu.with_memory_space_constraint(a, pltpu.HBM) for a in (lengths, q, k, v, g, o, norm)
    )
    return pl.pallas_call(
        gather_kernel,
        name="gather_heads",
        out_shape=(
            wide, wide, wide, wide,
            pltpu.VMEM((2, 6, 4, 128), jnp.float32),
            pltpu.VMEM((2, PLANE + PLANE // 2, 1, 128), jnp.float32),
            pltpu.VMEM((N_TILE, 1, TILE), jnp.int32),
            pltpu.SMEM((2 * N_TILE,), jnp.int32),
        ),
        in_specs=[pl.BlockSpec(memory_space=pltpu.HBM)] * 7,
        out_specs=[pl.BlockSpec(memory_space=pltpu.VMEM)] * 7 + [pl.BlockSpec(memory_space=pltpu.SMEM)],
        scratch_shapes=[
            pltpu.SMEM(lengths.shape, lengths.dtype),
            pltpu.VMEM(g.shape, g.dtype),
            pltpu.VMEM(o.shape, o.dtype),
            pltpu.VMEM(norm.shape, norm.dtype),
            pltpu.VMEM((heads // HEAD, 4, 128), jnp.float32),
            pltpu.VMEM((heads, 1, 128), jnp.float32),
            pltpu.SemaphoreType.DMA((2, 4)),
            pltpu.SemaphoreType.DMA((7,)),
            pltpu.SemaphoreType.DMA((2, X + 1)),
            pltpu.SemaphoreType.DMA((2, X, 2)),
            pltpu.SemaphoreType.DMA((2, X, 2)),
            pltpu.SemaphoreType.DMA((2, 2, 2)),
            pltpu.SemaphoreType.DMA((2, 2)),
            pltpu.SemaphoreType.DMA((4,)),
            pltpu.SemaphoreType.DMA((4,)),
            pltpu.SemaphoreType.DMA((4,)),
        ],
        compiler_params=pltpu.CompilerParams(has_side_effects=True, collective_id=0, vmem_limit_bytes=24 * 2**20),
    )(lengths, q, k, v, g, o, norm)


def attention_kernel(
    plan, q_ref, k_ref, v_ref, g_ref, lse_ref, delta_ref, start_t, dq_ref, dk_ref, dv_ref,
    dq_acc, dk_acc, dv_acc, lse_t, delta_t,
):
    scaling = 1.0 / math.sqrt(HD)

    z, x, head, _ = place()
    shared = shares(x, head)
    reach = plan[1]
    for j in range(1, N_TILE):
        reach = jnp.maximum(reach, plan[2 * j + 1])

    def begin_slot(s):
        for i in range(N_TILE):
            lse, delta = [], []
            for c in range(2 * i, 2 * i + 2):
                lse.append(lse_ref[s, c // 4, pl.ds(c % 4, 1), :] * LOG2E)
                delta.append(delta_ref[s, 2 * c] + delta_ref[s, 2 * c + 1])
            lse_t[s, i] = jnp.concatenate(lse, axis=1)
            delta_t[s, i] = jnp.concatenate(delta, axis=1)

        def clear(i, carry):
            dq_acc[s, i] = jnp.zeros((HD, TILE), jnp.float32)
            return carry

        lax.fori_loop(0, reach, clear, 0)

    def end_slot(s):
        def store(i, carry):
            query_rows = pl.ds(pl.multiple_of(i * TILE, TILE), TILE)
            dq_ref[s, query_rows] = (dq_acc[s, i] * scaling).T.astype(jnp.bfloat16)
            return carry

        def store_zero(i, carry):
            query_rows = pl.ds(pl.multiple_of(i * TILE, TILE), TILE)
            dq_ref[s, query_rows] = jnp.zeros((TILE, HD), jnp.bfloat16)
            return carry

        lax.fori_loop(0, reach, store, 0)
        lax.fori_loop(reach, N_TILE, store_zero, 0)

    def key_tile(j, carry):
        key_rows = pl.ds(pl.multiple_of(j * TILE, TILE), TILE)

        begin, end = plan[2 * j], plan[2 * j + 1]

        both = shared & (j % 2 == head % 2)
        alive = end > begin

        def skip(s):
            dk_ref[s, key_rows] = jnp.zeros((TILE, HD), jnp.bfloat16)
            dv_ref[s, key_rows] = jnp.zeros((TILE, HD), jnp.bfloat16)

        def work(slots):
            for s in slots:
                dk_acc[s] = jnp.zeros((TILE, HD), jnp.float32)
                dv_acc[s] = jnp.zeros((TILE, HD), jnp.float32)
            key_pos = j * TILE - HALO + lax.broadcasted_iota(jnp.int32, (TILE, 1), 0)
            keys = [k_ref[s, key_rows] for s in slots]
            values = [v_ref[s, key_rows] for s in slots]
            keys_t = [key.T for key in keys]

            def tiles(i, count):
                query_rows = pl.ds(pl.multiple_of(i * TILE, TILE), TILE * count)

                def along(read):
                    return jnp.concatenate([read(i + m) for m in range(count)], axis=1)

                query_pos = i * TILE + lax.broadcasted_iota(jnp.int32, (1, TILE * count), 1)
                live = (key_pos <= query_pos) & (key_pos >= along(lambda at: start_t[at]))
                raw = [
                    (
                        lax.dot_general(keys[s], q_ref[s, query_rows], NT, preferred_element_type=jnp.float32),
                        lax.dot_general(values[s], g_ref[s, query_rows], NT, preferred_element_type=jnp.float32),
                    )
                    for s in slots
                ]
                low = []
                for s in slots:
                    score, dweight = raw[s]
                    weight = jnp.exp2(score * (scaling * LOG2E) - along(lambda at: lse_t[s, at]))
                    weight = jnp.where(live, weight, 0.0)
                    dscore = weight * (dweight - along(lambda at: delta_t[s, at]))
                    low.append((weight.astype(jnp.bfloat16), dscore.astype(jnp.bfloat16)))
                for s in slots:
                    weight, dscore = low[s]
                    dv_acc[s] += jnp.dot(weight, g_ref[s, query_rows], preferred_element_type=jnp.float32)
                    dk_acc[s] += jnp.dot(dscore, q_ref[s, query_rows], preferred_element_type=jnp.float32)
                    for m in range(count):
                        part = dscore[:, m * TILE : (m + 1) * TILE]
                        dq_acc[s, i + m] += jnp.dot(keys_t[s], part, preferred_element_type=jnp.float32)

            def several(t, carry):
                tiles(begin + AT_ONCE * t, AT_ONCE)
                return carry

            def single(i, carry):
                tiles(i, 1)
                return carry

            groups = (end - begin) // AT_ONCE
            lax.fori_loop(0, groups, several, 0)
            lax.fori_loop(begin + AT_ONCE * groups, end, single, 0)
            for s in slots:
                dk_ref[s, key_rows] = (dk_acc[s] * scaling).astype(jnp.bfloat16)
                dv_ref[s, key_rows] = dv_acc[s].astype(jnp.bfloat16)

        @pl.when(alive & both)
        def _():
            work((0, 1))

        @pl.when(alive & jnp.logical_not(both))
        def _():
            work((0,))

        @pl.when(jnp.logical_not(alive))
        def _():
            skip(0)

        @pl.when(shared & jnp.logical_not(alive & both))
        def _():
            skip(1)

        return carry

    begin_slot(0)

    @pl.when(shared)
    def _():
        begin_slot(1)

    lax.fori_loop(0, N_TILE, key_tile, 0)
    end_slot(0)

    @pl.when(shared)
    def _():
        end_slot(1)


def attention(plan, q, k, v, g, lse, delta, start):
    shape = pltpu.VMEM((2, WIDE, HD), jnp.bfloat16)
    whole = pl.BlockSpec(memory_space=pltpu.VMEM)
    return pl.pallas_call(
        attention_kernel,
        name="attention_backward",
        out_shape=(shape, shape, shape),
        in_specs=[pl.BlockSpec(memory_space=pltpu.SMEM)] + [whole] * 7,
        out_specs=[whole] * 3,
        scratch_shapes=[
            pltpu.VMEM((2, N_TILE, HD, TILE), jnp.float32),
            pltpu.VMEM((2, TILE, HD), jnp.float32),
            pltpu.VMEM((2, TILE, HD), jnp.float32),
            pltpu.VMEM((2, N_TILE, 1, TILE), jnp.float32),
            pltpu.VMEM((2, N_TILE, 1, TILE), jnp.float32),
        ],
        compiler_params=pltpu.CompilerParams(vmem_limit_bytes=24 * 2**20),
    )(plan, q, k, v, g, lse, delta, start)


def scatter_kernel(
    dq_in, dk_in, dv_in, dq_out, dk_out, dv_out,
    halo, part, total, theirs, joined, send_sem, recv_sem, z_send, z_recv, load_sem, mate_send, mate_recv,
):
    z, x, head, p = place()
    owner, e_own = own_extra(x, head)
    up = {"ctx": ((z + 1) % Z) * X + x, "head": head}
    down = {"ctx": ((z + Z - 1) % Z) * X + x, "head": head}
    barrier = greet(z, x, head, p)
    half = PLANE // 2
    ins, outs, bases = (dq_in, dk_in, dv_in), (dq_out, dk_out, dv_out), (0, HALO, HALO)
    sent = (pl.ds(SPAN, HALO), pl.ds(0, HALO), pl.ds(0, HALO))
    kept = (pl.ds(0, HALO), pl.ds(SPAN, HALO), pl.ds(SPAN, HALO))

    helper = shares(x, head) & (head % 2 == 1)
    mate = {"ctx": z * X + x, "head": head // 2 * 2}

    def own(slot, n, at):
        return ins[n].at[0, at] if slot == 0 else joined.at[n, at]

    def join(n):
        await_bytes(theirs.at[n], mate_recv.at[n])

        def step(i, carry):
            at = pl.ds(pl.multiple_of(i * TILE, TILE), TILE)
            joined[n, at] = (ins[n][1, at].astype(jnp.float32) + theirs[n, at].astype(jnp.float32)).astype(jnp.bfloat16)
            return carry

        lax.fori_loop(0, N_TILE, step, 0)

    def exchange(slot):
        for n, device in ((1, down), (0, up), (2, down)):
            remote(own(slot, n, sent[n]), halo.at[slot, n], z_send.at[slot, n], z_recv.at[slot, n], device)
        for n in range(3):
            pltpu.make_async_copy(own(slot, n, kept[n]), part.at[slot, n], load_sem.at[slot, n]).start()

    def deliver(slot, at, n, src, peer):
        dst = outs[n].at[:, columns(at)]

        @pl.when(peer == p)
        def _():
            pltpu.make_async_copy(src, dst, recv_sem.at[n]).start()

        @pl.when(peer != p)
        def _():
            remote(src, dst, send_sem.at[slot, n], recv_sem.at[n], plane_device(z, peer))

    def combine(slot, n):
        await_bytes(part.at[slot, n], load_sem.at[slot, n])
        await_bytes(halo.at[slot, n], z_recv.at[slot, n])
        total[slot, n] = (part[slot, n].astype(jnp.float32) + halo[slot, n].astype(jnp.float32)).astype(jnp.bfloat16)

    def phase(slot, *halves):
        def send(slot, at):
            def step(i, carry):
                to_head = (head + turn(i)) % HEAD
                for c in range(2):
                    for n, upper, combined in halves:
                        near = (x + c) % 2 * HEAD + to_head
                        peer = upper * half + near
                        src = total.at[slot, n, rows(0, near)] if combined else own(slot, n, rows(bases[n], peer))
                        deliver(slot, at, n, src, peer)
                return carry

            lax.fori_loop(0, HEAD, step, 0)

        send(slot, p if slot == 0 else PLANE + e_own)

    def finish(slot):
        for n in range(3):
            await_bytes(halo.at[slot, n], z_send.at[slot, n])
            await_bytes(ins[n].at[slot, pl.ds(0, (PLANE - 1) * ROWS)], send_sem.at[slot, n])

    pl.semaphore_wait(barrier, PLANE + 1)
    @pl.when(helper)
    def _():
        for n in (1, 0, 2):
            remote(ins[n].at[1], theirs.at[n], mate_send.at[n], mate_recv.at[n], mate)

    early = (0, 1, False), (1, 0, False), (2, 0, False)
    exchange(0)
    phase(0, *early)

    @pl.when(owner)
    def _():
        for n in (1, 0, 2):
            join(n)
        exchange(1)
        phase(1, *early)

    for n, upper in ((1, 1), (0, 0), (2, 1)):
        combine(0, n)
        phase(0, (n, upper, True))

        @pl.when(owner)
        def _():
            combine(1, n)
            phase(1, (n, upper, True))

    @pl.when(helper)
    def _():
        for n in range(3):
            await_bytes(ins[n].at[1], mate_send.at[n])

    for n in range(3):
        await_bytes(outs[n], recv_sem.at[n])
    finish(0)

    @pl.when(owner)
    def _():
        finish(1)


def scatter(dq, dk, dv):
    shape = jax.ShapeDtypeStruct((ROWS, (PLANE + EXTRA) * HD), jnp.bfloat16)
    buffer = pltpu.VMEM((2, 3, HALO, HD), jnp.bfloat16)
    return pl.pallas_call(
        scatter_kernel,
        name="scatter_heads",
        out_shape=(shape, shape, shape),
        in_specs=[pl.BlockSpec(memory_space=pltpu.VMEM)] * 3,
        out_specs=[pl.BlockSpec(memory_space=pl.ANY)] * 3,
        scratch_shapes=[
            buffer, buffer, buffer,
            pltpu.VMEM((3, WIDE, HD), jnp.bfloat16),
            pltpu.VMEM((3, WIDE, HD), jnp.bfloat16),
            pltpu.SemaphoreType.DMA((2, 3)),
            pltpu.SemaphoreType.DMA((3,)),
            pltpu.SemaphoreType.DMA((2, 3)),
            pltpu.SemaphoreType.DMA((2, 3)),
            pltpu.SemaphoreType.DMA((2, 3)),
            pltpu.SemaphoreType.DMA((3,)),
            pltpu.SemaphoreType.DMA((3,)),
        ],
        compiler_params=pltpu.CompilerParams(has_side_effects=True, collective_id=1, vmem_limit_bytes=24 * 2**20),
    )(dq, dk, dv)


def on_device(queries, keys, values, outputs, out_grad, log_norms, doc_lengths):
    q, k, v, g, lse, delta, start, plan = gather(
        doc_lengths, queries, keys, values, out_grad, outputs, log_norms.T
    )
    dq, dk, dv = attention(plan, q, k, v, g, lse, delta, start)
    return scatter(dq, dk, dv)


def solution(mesh):
    row = P(("ctx", "head"), None)
    return jax.shard_map(
        on_device,
        mesh=mesh,
        in_specs=(row, row, row, row, row, P("ctx", "head"), P()),
        out_specs=(row, row, row),
        check_vma=False,
    )
```

```python
import math

import jax
import jax.numpy as jnp
from jax import lax
from jax.experimental import pallas as pl
from jax.experimental.pallas import tpu as pltpu
from jax.sharding import PartitionSpec as P

NT = (((1,), (1,)), ((), ()))
MESH = pl.DeviceIdType.MESH
HD = 128
X, HEAD, Z = 4, 8, 8
PLANE = X * HEAD
ROWS = 64
SPAN = PLANE * ROWS
HALO = SPAN // 2
WIDE = SPAN + HALO
EXTRA = 8
TILE = 256
N_TILE = WIDE // TILE
AT_ONCE = 3
DOCS = 16
LOG2E = math.log2(math.e)


def place():
    ctx, head = lax.axis_index("ctx"), lax.axis_index("head")
    z, x = ctx // X, ctx % X
    return z, x, head, x * HEAD + head


def extra_owner(e):
    x = e // 2
    return x * HEAD + (2 * (e % 2) + x % 2) * 2


def own_extra(x, head):
    y, core = head // 2, head % 2
    return (core == 0) & ((x + y) % 2 == 0), x * 2 + y // 2


def shares(x, head):
    return (x + head // 2) % 2 == 0


def plane_device(z, peer):
    return {"ctx": z * X + peer // HEAD, "head": peer % HEAD}


def turn(i):
    return (2 + 4 * (i % 2) + 2 * (i // 2 % 2) + i // 4) % HEAD


def columns(head):
    return pl.ds(pl.multiple_of(head * HD, HD), HD)


def rows(base, peer):
    return pl.ds(pl.multiple_of(base + peer * ROWS, ROWS), ROWS)


def greet(z, x, head, p):
    barrier = pltpu.get_barrier_semaphore()

    for i in range(1, PLANE):
        pl.semaphore_signal(barrier, inc=1, device_id=plane_device(z, (p + i) % PLANE), device_id_type=MESH)
    for step in (1, Z - 1):
        pl.semaphore_signal(barrier, inc=1, device_id={"ctx": ((z + step) % Z) * X + x, "head": head}, device_id_type=MESH)
    return barrier


def remote(src, dst, send, recv, device):
    pltpu.make_async_remote_copy(
        src_ref=src, dst_ref=dst, send_sem=send, recv_sem=recv, device_id=device, device_id_type=MESH
    ).start()


def await_bytes(ref, sem):
    pltpu.make_async_copy(ref, ref, sem).wait()


def local_statistics(p, grad, output, norm, lse, delta):
    heads = delta.shape[0]
    product = grad[...].astype(jnp.float32) * output[...].astype(jnp.float32)
    high = product.astype(jnp.bfloat16)
    low = (product - high.astype(jnp.float32)).astype(jnp.bfloat16)
    head_of = lax.broadcasted_iota(jnp.int32, (heads, heads * HD), 1) // HD
    select = jnp.where(head_of == lax.broadcasted_iota(jnp.int32, (heads, heads * HD), 0), 1.0, 0.0).astype(jnp.bfloat16)
    sums = lax.dot_general(select, high, NT, preferred_element_type=jnp.float32)
    sums += lax.dot_general(select, low, NT, preferred_element_type=jnp.float32)
    empty = jnp.zeros_like(sums)
    wide = jnp.where(p % 2 == 0, jnp.concatenate([sums, empty], axis=1), jnp.concatenate([empty, sums], axis=1))
    for h in range(heads):
        delta[h] = wide[h : h + 1]
    for j in range(lse.shape[0]):
        for c in range(4):
            lse[j, pl.ds(c, 1), :] = norm[pl.ds(j, 1), pl.ds(c * 128, 128)]


def prepare(z, lengths, plan, start_t):
    starts, ends, at = [], [], -z * SPAN
    for d in range(DOCS):
        starts.append(at)
        at = at + lengths[d]
        ends.append(at)
    take_low, take_high = jnp.int32(0), jnp.int32(0)
    for start, end in zip(starts, ends):
        take_low = take_low | ((start < 0) & (end > 0) & (start >= -HALO)).astype(jnp.int32)
        take_high = take_high | ((start < SPAN) & (end > SPAN) & (start < SPAN - HALO)).astype(jnp.int32)
    for j in range(N_TILE):
        first = j * TILE - HALO
        last = first + TILE - 1
        end_last = jnp.int32(1 << 20)
        for end in reversed(ends):
            end_last = jnp.where(end > last, end, end_last)
        limit = jnp.where(take_low > 0, SPAN, 0) if first < 0 else jnp.where(take_high > 0, WIDE, SPAN)
        low = jnp.int32(max(first, 0) // TILE)
        plan[2 * j] = low
        plan[2 * j + 1] = jnp.maximum((jnp.maximum(jnp.minimum(end_last, limit), 0) + TILE - 1) // TILE, low)
    for i in range(N_TILE):
        pos = i * TILE + lax.broadcasted_iota(jnp.int32, (1, TILE), 1)
        own = jnp.full((1, TILE), -(1 << 20), jnp.int32)
        for start in starts:
            own = jnp.where(pos >= start, start, own)
        start_t[i] = own


def gather_kernel(
    lengths_in, q_in, k_in, v_in, g_in, o_in, norm_in,
    q_out, k_out, v_out, g_out, lse_out, delta_out, start_out, plan_out,
    lengths, grad, output, norm, lse_in, delta_in,
    send_sem, stat_send, recv_sem, z_send, z_recv, z_stat, stat_recv, load_sem, mate_send, mate_recv,
):
    z, x, head, p = place()
    owner, e_own = own_extra(x, head)
    barrier = greet(z, x, head, p)
    loads = [
        pltpu.make_async_copy(src, dst, load_sem.at[n])
        for n, (src, dst) in enumerate(((g_in, grad), (o_in, output), (norm_in, norm), (lengths_in, lengths)))
    ]
    for load in loads:
        load.start()
    helper = shares(x, head) & (head % 2 == 1)
    mate = {"ctx": z * X + x, "head": head // 2 * 2 + 1}
    lower = p < PLANE // 2
    up = {"ctx": ((z + 1) % Z) * X + x, "head": head}
    down = {"ctx": ((z + Z - 1) % Z) * X + x, "head": head}
    pl.semaphore_wait(barrier, PLANE + 1)

    query_side = ((0, q_in, q_out, 0), (3, g_in, g_out, 0))
    key_side = ((1, k_in, k_out, HALO), (2, v_in, v_out, HALO))
    rest = X

    def scatter(side, group, away, extra_away, begin, end):
        def step(i, carry):
            for d in away:
                to_x = (x + d) % X
                peer = to_x * HEAD + (head + turn((i + 2 * d) % HEAD)) % HEAD
                for n, src, dst, base in side:
                    from_, to = src.at[:, columns(peer)], dst.at[0, rows(base, p)]

                    @pl.when(peer == p)
                    def _():
                        pltpu.make_async_copy(from_, to, recv_sem.at[0, group]).start()

                    @pl.when(peer != p)
                    def _():
                        remote(from_, to, send_sem.at[0, n], recv_sem.at[0, group], plane_device(z, peer))

            for d in extra_away:

                @pl.when((i % 2 == 0) & (i < 4))
                def _():
                    e = (x + d) % X * 2 + i // 2
                    extra = extra_owner(e)
                    for n, src, dst, base in side:
                        from_, to = src.at[:, columns(PLANE + e)], dst.at[1, rows(base, p)]

                        @pl.when(extra == p)
                        def _():
                            pltpu.make_async_copy(from_, to, recv_sem.at[1, group]).start()

                        @pl.when(extra != p)
                        def _():
                            remote(from_, to, send_sem.at[1, n], recv_sem.at[1, group], plane_device(z, extra))

            return carry

        lax.fori_loop(begin, end, step, 0)

    def scatter_first(away, extra_away, begin=0, end=HEAD):
        @pl.when(lower)
        def _():
            scatter(query_side, x, away, extra_away, begin, end)

        @pl.when(jnp.logical_not(lower))
        def _():
            scatter(key_side, x, away, extra_away, begin, end)

    def scatter_rest(away, extra_away, begin=0, end=HEAD):
        @pl.when(lower)
        def _():
            scatter(key_side, rest, away, extra_away, begin, end)

        @pl.when(jnp.logical_not(lower))
        def _():
            scatter(query_side, rest, away, extra_away, begin, end)

    block = SPAN // X
    stats = (
        (0, lse_out, pl.ds(0, 2), pl.ds(X, 2)),
        (1, delta_out, pl.ds(0, PLANE // 2), pl.ds(PLANE, PLANE // 2)),
    )

    def forward_stats(slot):
        await_bytes(lse_out.at[slot, pl.ds(0, X)], stat_recv.at[0, slot])
        await_bytes(delta_out.at[slot, pl.ds(0, PLANE)], stat_recv.at[1, slot])
        for n, ref, near, far in stats:
            remote(ref.at[slot, near], ref.at[slot, far], z_stat.at[0, slot, n], z_stat.at[1, slot, n], down)

    def pieces(xs):
        here = pl.ds(pl.multiple_of(HALO + xs * block, block), block)
        there = pl.ds(pl.multiple_of((xs - X // 2) * block, block), block)
        low_here = pl.ds(pl.multiple_of(xs * block, block), block)
        low_there = pl.ds(pl.multiple_of(SPAN + xs * block, block), block)
        return ((k_out, here, there), (v_out, here, there)), ((q_out, low_here, low_there), (g_out, low_here, low_there))

    def hand_over(ref, here, kind):
        remote(ref.at[1, here], ref.at[1, here], mate_send.at[kind], mate_recv.at[kind], mate)

    def forward(slot, xs):
        await_bytes(k_out.at[slot, pl.ds(0, 2 * block)], recv_sem.at[slot, xs])
        keys, queries = pieces(xs)
        if slot == 1:

            @pl.when(xs >= X // 2)
            def _():
                for ref, here, there in keys:
                    hand_over(ref, here, 0)

            @pl.when(xs < X // 2)
            def _():
                for ref, here, there in queries:
                    hand_over(ref, here, 1)

        @pl.when(xs >= X // 2)
        def _():
            for n, (ref, here, there) in enumerate(keys):
                remote(ref.at[slot, here], ref.at[slot, there], z_send.at[slot, xs, n], z_recv.at[slot, xs, n], up)

        @pl.when(xs < X // 2)
        def _():
            for n, (ref, here, there) in enumerate(queries):
                remote(ref.at[slot, here], ref.at[slot, there], z_send.at[slot, xs, n], z_recv.at[slot, xs, n], down)

    sides, ends = (1, 3), (2, 0)

    def finish(slot):
        await_bytes(k_out.at[:, pl.ds(0, 2 * HALO)], recv_sem.at[slot, rest])
        if slot == 1:
            for ref in (k_out, v_out):
                hand_over(ref, pl.ds(HALO, HALO), 0)
            for ref in (q_out, g_out):
                hand_over(ref, pl.ds(HALO, HALO), 1)
        for d in sides + ends:
            xs = (x + X - d) % X
            for n in range(2):
                await_bytes(k_out.at[slot, pl.ds(0, block)], z_recv.at[slot, xs, n])
                await_bytes(k_out.at[slot, pl.ds(0, block)], z_send.at[slot, xs, n])
            if slot == 1:
                keys, queries = pieces(xs)

                @pl.when(xs >= X // 2)
                def _():
                    for ref, here, there in keys:
                        hand_over(ref, there, 0)

                @pl.when(xs < X // 2)
                def _():
                    for ref, here, there in queries:
                        hand_over(ref, there, 1)

        for n, ref, near, far in stats:
            await_bytes(ref.at[slot, near], z_stat.at[0, slot, n])
            await_bytes(ref.at[slot, far], z_stat.at[1, slot, n])
        if slot == 1:
            hand_over(lse_out, pl.ds(0, X + 2), 2)
            hand_over(delta_out, pl.ds(0, PLANE + PLANE // 2), 3)

    def handed_over(sems):
        await_bytes(k_out, sems.at[0])
        await_bytes(q_out, sems.at[1])
        await_bytes(lse_out.at[1], sems.at[2])
        await_bytes(delta_out.at[1], sems.at[3])

    def forward_from(slot, away):
        for d in away:
            forward(slot, (x + X - d) % X)

    scatter_first(sides + ends, sides + ends, 0, 4)
    scatter_first(sides + ends, (), 4, 6)
    for load in loads:
        load.wait()
    local_statistics(p, grad, output, norm, lse_in, delta_in)

    @pl.when(owner)
    def _():
        forward_from(1, sides + ends)

    scatter_first(sides + ends, (), 6, HEAD)
    forward_from(0, sides)
    for j in range(5):
        h = head * 5 + j
        slot = h // PLANE
        target = jnp.where(h < PLANE, h, extra_owner(h - PLANE))
        src, dst = lse_in.at[j], lse_out.at[slot, x]

        @pl.when(target == p)
        def _():
            pltpu.make_async_copy(src, dst, stat_recv.at[0, slot]).start()

        @pl.when(target != p)
        def _():
            remote(src, dst, stat_send.at[j], stat_recv.at[0, slot], plane_device(z, target))

    def delta_main(i, carry):
        peer = (p + i) % PLANE
        remote(delta_in.at[peer], delta_out.at[0, p], stat_send.at[5], stat_recv.at[1, 0], plane_device(z, peer))
        return carry

    lax.fori_loop(1, PLANE, delta_main, 0)
    pltpu.make_async_copy(delta_in.at[p], delta_out.at[0, p], stat_recv.at[1, 0]).start()

    def delta_extra(e, carry):
        peer = extra_owner(e)
        src, dst = delta_in.at[PLANE + e], delta_out.at[1, p]

        @pl.when(peer == p)
        def _():
            pltpu.make_async_copy(src, dst, stat_recv.at[1, 1]).start()

        @pl.when(peer != p)
        def _():
            remote(src, dst, stat_send.at[6], stat_recv.at[1, 1], plane_device(z, peer))

        return carry

    lax.fori_loop(0, EXTRA, delta_extra, 0)

    scatter_rest(sides + ends, sides + ends, 0, HEAD // 2)
    forward_from(0, ends)
    scatter_rest(sides + ends, (), HEAD // 2, HEAD)
    prepare(z, lengths, plan_out, start_out)
    forward_stats(0)

    @pl.when(owner)
    def _():
        forward_stats(1)

    @pl.when(owner)
    def _():
        finish(1)

    finish(0)

    @pl.when(owner)
    def _():
        handed_over(mate_send)

    @pl.when(helper)
    def _():
        handed_over(mate_recv)

    for j in range(5):
        h = head * 5 + j
        target = jnp.where(h < PLANE, h, extra_owner(h - PLANE))

        @pl.when(target != p)
        def _():
            await_bytes(lse_in.at[j], stat_send.at[j])

    await_bytes(delta_in.at[pl.ds(0, PLANE - 1)], stat_send.at[5])
    for n in range(4):
        await_bytes(k_out.at[0, pl.ds(0, (PLANE - 1) * ROWS)], send_sem.at[0, n])

    @pl.when(owner)
    def _():
        await_bytes(delta_in.at[pl.ds(0, EXTRA - 1)], stat_send.at[6])
        for n in range(4):
            await_bytes(k_out.at[0, pl.ds(0, (EXTRA - 1) * ROWS)], send_sem.at[1, n])

    @pl.when(jnp.logical_not(owner))
    def _():
        await_bytes(delta_in.at[pl.ds(0, EXTRA)], stat_send.at[6])
        for n in range(4):
            await_bytes(k_out.at[0, pl.ds(0, EXTRA * ROWS)], send_sem.at[1, n])


def gather(lengths, q, k, v, g, o, norm):
    wide = pltpu.VMEM((2, WIDE, HD), jnp.bfloat16)
    heads = PLANE + EXTRA
    lengths, q, k, v, g, o, norm = (
        pltpu.with_memory_space_constraint(a, pltpu.HBM) for a in (lengths, q, k, v, g, o, norm)
    )
    return pl.pallas_call(
        gather_kernel,
        name="gather_heads",
        out_shape=(
            wide, wide, wide, wide,
            pltpu.VMEM((2, 6, 4, 128), jnp.float32),
            pltpu.VMEM((2, PLANE + PLANE // 2, 1, 128), jnp.float32),
            pltpu.VMEM((N_TILE, 1, TILE), jnp.int32),
            pltpu.SMEM((2 * N_TILE,), jnp.int32),
        ),
        in_specs=[pl.BlockSpec(memory_space=pltpu.HBM)] * 7,
        out_specs=[pl.BlockSpec(memory_space=pltpu.VMEM)] * 7 + [pl.BlockSpec(memory_space=pltpu.SMEM)],
        scratch_shapes=[
            pltpu.SMEM(lengths.shape, lengths.dtype),
            pltpu.VMEM(g.shape, g.dtype),
            pltpu.VMEM(o.shape, o.dtype),
            pltpu.VMEM(norm.shape, norm.dtype),
            pltpu.VMEM((heads // HEAD, 4, 128), jnp.float32),
            pltpu.VMEM((heads, 1, 128), jnp.float32),
            pltpu.SemaphoreType.DMA((2, 4)),
            pltpu.SemaphoreType.DMA((7,)),
            pltpu.SemaphoreType.DMA((2, X + 1)),
            pltpu.SemaphoreType.DMA((2, X, 2)),
            pltpu.SemaphoreType.DMA((2, X, 2)),
            pltpu.SemaphoreType.DMA((2, 2, 2)),
            pltpu.SemaphoreType.DMA((2, 2)),
            pltpu.SemaphoreType.DMA((4,)),
            pltpu.SemaphoreType.DMA((4,)),
            pltpu.SemaphoreType.DMA((4,)),
        ],
        compiler_params=pltpu.CompilerParams(has_side_effects=True, collective_id=0, vmem_limit_bytes=24 * 2**20),
    )(lengths, q, k, v, g, o, norm)


def attention_kernel(
    plan, q_ref, k_ref, v_ref, g_ref, lse_ref, delta_ref, start_t, dq_ref, dk_ref, dv_ref,
    dq_acc, dk_acc, dv_acc, lse_t, delta_t,
):
    scaling = 1.0 / math.sqrt(HD)

    z, x, head, _ = place()
    shared = shares(x, head)
    reach = plan[1]
    for j in range(1, N_TILE):
        reach = jnp.maximum(reach, plan[2 * j + 1])

    def begin_slot(s):
        for i in range(N_TILE):
            lse, delta = [], []
            for c in range(2 * i, 2 * i + 2):
                lse.append(lse_ref[s, c // 4, pl.ds(c % 4, 1), :] * LOG2E)
                delta.append(delta_ref[s, 2 * c] + delta_ref[s, 2 * c + 1])
            lse_t[s, i] = jnp.concatenate(lse, axis=1)
            delta_t[s, i] = jnp.concatenate(delta, axis=1)

        def clear(i, carry):
            dq_acc[s, i] = jnp.zeros((HD, TILE), jnp.float32)
            return carry

        lax.fori_loop(0, reach, clear, 0)

    def end_slot(s):
        def store(i, carry):
            query_rows = pl.ds(pl.multiple_of(i * TILE, TILE), TILE)
            dq_ref[s, query_rows] = (dq_acc[s, i] * scaling).T.astype(jnp.bfloat16)
            return carry

        def store_zero(i, carry):
            query_rows = pl.ds(pl.multiple_of(i * TILE, TILE), TILE)
            dq_ref[s, query_rows] = jnp.zeros((TILE, HD), jnp.bfloat16)
            return carry

        lax.fori_loop(0, reach, store, 0)
        lax.fori_loop(reach, N_TILE, store_zero, 0)

    def key_tile(j, carry):
        key_rows = pl.ds(pl.multiple_of(j * TILE, TILE), TILE)

        begin, end = plan[2 * j], plan[2 * j + 1]

        both = shared & (j % 2 == head % 2)
        alive = end > begin

        def skip(s):
            dk_ref[s, key_rows] = jnp.zeros((TILE, HD), jnp.bfloat16)
            dv_ref[s, key_rows] = jnp.zeros((TILE, HD), jnp.bfloat16)

        def work(slots):
            for s in slots:
                dk_acc[s] = jnp.zeros((TILE, HD), jnp.float32)
                dv_acc[s] = jnp.zeros((TILE, HD), jnp.float32)
            key_pos = j * TILE - HALO + lax.broadcasted_iota(jnp.int32, (TILE, 1), 0)
            keys = [k_ref[s, key_rows] for s in slots]
            values = [v_ref[s, key_rows] for s in slots]
            keys_t = [key.T for key in keys]

            def tiles(i, count):
                query_rows = pl.ds(pl.multiple_of(i * TILE, TILE), TILE * count)

                def along(read):
                    return jnp.concatenate([read(i + m) for m in range(count)], axis=1)

                query_pos = i * TILE + lax.broadcasted_iota(jnp.int32, (1, TILE * count), 1)
                live = (key_pos <= query_pos) & (key_pos >= along(lambda at: start_t[at]))
                raw = [
                    (
                        lax.dot_general(keys[s], q_ref[s, query_rows], NT, preferred_element_type=jnp.float32),
                        lax.dot_general(values[s], g_ref[s, query_rows], NT, preferred_element_type=jnp.float32),
                    )
                    for s in slots
                ]
                low = []
                for s in slots:
                    score, dweight = raw[s]
                    weight = jnp.exp2(score * (scaling * LOG2E) - along(lambda at: lse_t[s, at]))
                    weight = jnp.where(live, weight, 0.0)
                    dscore = weight * (dweight - along(lambda at: delta_t[s, at]))
                    low.append((weight.astype(jnp.bfloat16), dscore.astype(jnp.bfloat16)))
                for s in slots:
                    weight, dscore = low[s]
                    dv_acc[s] += jnp.dot(weight, g_ref[s, query_rows], preferred_element_type=jnp.float32)
                    dk_acc[s] += jnp.dot(dscore, q_ref[s, query_rows], preferred_element_type=jnp.float32)
                    for m in range(count):
                        part = dscore[:, m * TILE : (m + 1) * TILE]
                        dq_acc[s, i + m] += jnp.dot(keys_t[s], part, preferred_element_type=jnp.float32)

            def several(t, carry):
                tiles(begin + AT_ONCE * t, AT_ONCE)
                return carry

            def single(i, carry):
                tiles(i, 1)
                return carry

            groups = (end - begin) // AT_ONCE
            lax.fori_loop(0, groups, several, 0)
            lax.fori_loop(begin + AT_ONCE * groups, end, single, 0)
            for s in slots:
                dk_ref[s, key_rows] = (dk_acc[s] * scaling).astype(jnp.bfloat16)
                dv_ref[s, key_rows] = dv_acc[s].astype(jnp.bfloat16)

        @pl.when(alive & both)
        def _():
            work((0, 1))

        @pl.when(alive & jnp.logical_not(both))
        def _():
            work((0,))

        @pl.when(jnp.logical_not(alive))
        def _():
            skip(0)

        @pl.when(shared & jnp.logical_not(alive & both))
        def _():
            skip(1)

        return carry

    begin_slot(0)

    @pl.when(shared)
    def _():
        begin_slot(1)

    lax.fori_loop(0, N_TILE, key_tile, 0)
    end_slot(0)

    @pl.when(shared)
    def _():
        end_slot(1)


def attention(plan, q, k, v, g, lse, delta, start):
    shape = pltpu.VMEM((2, WIDE, HD), jnp.bfloat16)
    whole = pl.BlockSpec(memory_space=pltpu.VMEM)
    return pl.pallas_call(
        attention_kernel,
        name="attention_backward",
        out_shape=(shape, shape, shape),
        in_specs=[pl.BlockSpec(memory_space=pltpu.SMEM)] + [whole] * 7,
        out_specs=[whole] * 3,
        scratch_shapes=[
            pltpu.VMEM((2, N_TILE, HD, TILE), jnp.float32),
            pltpu.VMEM((2, TILE, HD), jnp.float32),
            pltpu.VMEM((2, TILE, HD), jnp.float32),
            pltpu.VMEM((2, N_TILE, 1, TILE), jnp.float32),
            pltpu.VMEM((2, N_TILE, 1, TILE), jnp.float32),
        ],
        compiler_params=pltpu.CompilerParams(vmem_limit_bytes=24 * 2**20),
    )(plan, q, k, v, g, lse, delta, start)


def scatter_kernel(
    dq_in, dk_in, dv_in, dq_out, dk_out, dv_out,
    halo, part, total, theirs, joined, send_sem, recv_sem, z_send, z_recv, load_sem, mate_send, mate_recv,
):
    z, x, head, p = place()
    owner, e_own = own_extra(x, head)
    up = {"ctx": ((z + 1) % Z) * X + x, "head": head}
    down = {"ctx": ((z + Z - 1) % Z) * X + x, "head": head}
    barrier = greet(z, x, head, p)
    half = PLANE // 2
    ins, outs, bases = (dq_in, dk_in, dv_in), (dq_out, dk_out, dv_out), (0, HALO, HALO)
    sent = (pl.ds(SPAN, HALO), pl.ds(0, HALO), pl.ds(0, HALO))
    kept = (pl.ds(0, HALO), pl.ds(SPAN, HALO), pl.ds(SPAN, HALO))

    helper = shares(x, head) & (head % 2 == 1)
    mate = {"ctx": z * X + x, "head": head // 2 * 2}

    def own(slot, n, at):
        return ins[n].at[0, at] if slot == 0 else joined.at[n, at]

    def join(n):
        await_bytes(theirs.at[n], mate_recv.at[n])

        def step(i, carry):
            at = pl.ds(pl.multiple_of(i * TILE, TILE), TILE)
            joined[n, at] = (ins[n][1, at].astype(jnp.float32) + theirs[n, at].astype(jnp.float32)).astype(jnp.bfloat16)
            return carry

        lax.fori_loop(0, N_TILE, step, 0)

    def exchange(slot):
        for n, device in ((1, down), (0, up), (2, down)):
            remote(own(slot, n, sent[n]), halo.at[slot, n], z_send.at[slot, n], z_recv.at[slot, n], device)
        for n in range(3):
            pltpu.make_async_copy(own(slot, n, kept[n]), part.at[slot, n], load_sem.at[slot, n]).start()

    def deliver(slot, at, n, src, peer):
        dst = outs[n].at[:, columns(at)]

        @pl.when(peer == p)
        def _():
            pltpu.make_async_copy(src, dst, recv_sem.at[n]).start()

        @pl.when(peer != p)
        def _():
            remote(src, dst, send_sem.at[slot, n], recv_sem.at[n], plane_device(z, peer))

    def combine(slot, n):
        await_bytes(part.at[slot, n], load_sem.at[slot, n])
        await_bytes(halo.at[slot, n], z_recv.at[slot, n])
        total[slot, n] = (part[slot, n].astype(jnp.float32) + halo[slot, n].astype(jnp.float32)).astype(jnp.bfloat16)

    def phase(slot, *halves):
        def send(slot, at):
            def step(i, carry):
                to_head = (head + turn(i)) % HEAD
                for c in range(2):
                    for n, upper, combined in halves:
                        near = (x + c) % 2 * HEAD + to_head
                        peer = upper * half + near
                        src = total.at[slot, n, rows(0, near)] if combined else own(slot, n, rows(bases[n], peer))
                        deliver(slot, at, n, src, peer)
                return carry

            lax.fori_loop(0, HEAD, step, 0)

        send(slot, p if slot == 0 else PLANE + e_own)

    def finish(slot):
        for n in range(3):
            await_bytes(halo.at[slot, n], z_send.at[slot, n])
            await_bytes(ins[n].at[slot, pl.ds(0, (PLANE - 1) * ROWS)], send_sem.at[slot, n])

    pl.semaphore_wait(barrier, PLANE + 1)
    @pl.when(helper)
    def _():
        for n in (1, 0, 2):
            remote(ins[n].at[1], theirs.at[n], mate_send.at[n], mate_recv.at[n], mate)

    early = (0, 1, False), (1, 0, False), (2, 0, False)
    exchange(0)
    phase(0, *early)

    @pl.when(owner)
    def _():
        for n in (1, 0, 2):
            join(n)
        exchange(1)
        phase(1, *early)

    for n, upper in ((1, 1), (0, 0), (2, 1)):
        combine(0, n)
        phase(0, (n, upper, True))

        @pl.when(owner)
        def _():
            combine(1, n)
            phase(1, (n, upper, True))

    @pl.when(helper)
    def _():
        for n in range(3):
            await_bytes(ins[n].at[1], mate_send.at[n])

    for n in range(3):
        await_bytes(outs[n], recv_sem.at[n])
    finish(0)

    @pl.when(owner)
    def _():
        finish(1)


def scatter(dq, dk, dv):
    shape = jax.ShapeDtypeStruct((ROWS, (PLANE + EXTRA) * HD), jnp.bfloat16)
    buffer = pltpu.VMEM((2, 3, HALO, HD), jnp.bfloat16)
    return pl.pallas_call(
        scatter_kernel,
        name="scatter_heads",
        out_shape=(shape, shape, shape),
        in_specs=[pl.BlockSpec(memory_space=pltpu.VMEM)] * 3,
        out_specs=[pl.BlockSpec(memory_space=pl.ANY)] * 3,
        scratch_shapes=[
            buffer, buffer, buffer,
            pltpu.VMEM((3, WIDE, HD), jnp.bfloat16),
            pltpu.VMEM((3, WIDE, HD), jnp.bfloat16),
            pltpu.SemaphoreType.DMA((2, 3)),
            pltpu.SemaphoreType.DMA((3,)),
            pltpu.SemaphoreType.DMA((2, 3)),
            pltpu.SemaphoreType.DMA((2, 3)),
            pltpu.SemaphoreType.DMA((2, 3)),
            pltpu.SemaphoreType.DMA((3,)),
            pltpu.SemaphoreType.DMA((3,)),
        ],
        compiler_params=pltpu.CompilerParams(has_side_effects=True, collective_id=1, vmem_limit_bytes=24 * 2**20),
    )(dq, dk, dv)


def on_device(queries, keys, values, outputs, out_grad, log_norms, doc_lengths):
    q, k, v, g, lse, delta, start, plan = gather(
        doc_lengths, queries, keys, values, out_grad, outputs, log_norms.T
    )
    dq, dk, dv = attention(plan, q, k, v, g, lse, delta, start)
    return scatter(dq, dk, dv)


def solution(mesh):
    row = P(("ctx", "head"), None)
    return jax.shard_map(
        on_device,
        mesh=mesh,
        in_specs=(row, row, row, row, row, P("ctx", "head"), P()),
        out_specs=(row, row, row),
        check_vma=False,
    )
```

```python
import math

import jax
import jax.numpy as jnp
from jax import lax
from jax.experimental import pallas as pl
from jax.experimental.pallas import tpu as pltpu
from jax.sharding import PartitionSpec as P

NT = (((1,), (1,)), ((), ()))
MESH = pl.DeviceIdType.MESH
HD = 128
X, HEAD, Z = 4, 8, 8
PLANE = X * HEAD
ROWS = 64
SPAN = PLANE * ROWS
HALO = SPAN // 2
WIDE = SPAN + HALO
EXTRA = 8
TILE = 256
N_TILE = WIDE // TILE
AT_ONCE = 3
DOCS = 16
LOG2E = math.log2(math.e)


def place():
    ctx, head = lax.axis_index("ctx"), lax.axis_index("head")
    z, x = ctx // X, ctx % X
    return z, x, head, x * HEAD + head


def extra_owner(e):
    x = e // 2
    return x * HEAD + (2 * (e % 2) + x % 2) * 2


def own_extra(x, head):
    y, core = head // 2, head % 2
    return (core == 0) & ((x + y) % 2 == 0), x * 2 + y // 2


def shares(x, head):
    return (x + head // 2) % 2 == 0


def plane_device(z, peer):
    return {"ctx": z * X + peer // HEAD, "head": peer % HEAD}


def turn(i):
    return (2 + 4 * (i % 2) + 2 * (i // 2 % 2) + i // 4) % HEAD


def columns(head):
    return pl.ds(pl.multiple_of(head * HD, HD), HD)


def rows(base, peer):
    return pl.ds(pl.multiple_of(base + peer * ROWS, ROWS), ROWS)


def greet(z, x, head, p):
    barrier = pltpu.get_barrier_semaphore()

    for i in range(1, PLANE):
        pl.semaphore_signal(barrier, inc=1, device_id=plane_device(z, (p + i) % PLANE), device_id_type=MESH)
    for step in (1, Z - 1):
        pl.semaphore_signal(barrier, inc=1, device_id={"ctx": ((z + step) % Z) * X + x, "head": head}, device_id_type=MESH)
    return barrier


def remote(src, dst, send, recv, device):
    pltpu.make_async_remote_copy(
        src_ref=src, dst_ref=dst, send_sem=send, recv_sem=recv, device_id=device, device_id_type=MESH
    ).start()


def await_bytes(ref, sem):
    pltpu.make_async_copy(ref, ref, sem).wait()


def local_statistics(p, grad, output, norm, lse, delta):
    heads = delta.shape[0]
    product = grad[...].astype(jnp.float32) * output[...].astype(jnp.float32)
    high = product.astype(jnp.bfloat16)
    low = (product - high.astype(jnp.float32)).astype(jnp.bfloat16)
    head_of = lax.broadcasted_iota(jnp.int32, (heads, heads * HD), 1) // HD
    select = jnp.where(head_of == lax.broadcasted_iota(jnp.int32, (heads, heads * HD), 0), 1.0, 0.0).astype(jnp.bfloat16)
    sums = lax.dot_general(select, high, NT, preferred_element_type=jnp.float32)
    sums += lax.dot_general(select, low, NT, preferred_element_type=jnp.float32)
    empty = jnp.zeros_like(sums)
    wide = jnp.where(p % 2 == 0, jnp.concatenate([sums, empty], axis=1), jnp.concatenate([empty, sums], axis=1))
    for h in range(heads):
        delta[h] = wide[h : h + 1]
    for j in range(lse.shape[0]):
        for c in range(4):
            lse[j, pl.ds(c, 1), :] = norm[pl.ds(j, 1), pl.ds(c * 128, 128)]


def prepare(z, lengths, plan, start_t):
    starts, ends, at = [], [], -z * SPAN
    for d in range(DOCS):
        starts.append(at)
        at = at + lengths[d]
        ends.append(at)
    take_low, take_high = jnp.int32(0), jnp.int32(0)
    for start, end in zip(starts, ends):
        take_low = take_low | ((start < 0) & (end > 0) & (start >= -HALO)).astype(jnp.int32)
        take_high = take_high | ((start < SPAN) & (end > SPAN) & (start < SPAN - HALO)).astype(jnp.int32)
    for j in range(N_TILE):
        first = j * TILE - HALO
        last = first + TILE - 1
        end_last = jnp.int32(1 << 20)
        for end in reversed(ends):
            end_last = jnp.where(end > last, end, end_last)
        limit = jnp.where(take_low > 0, SPAN, 0) if first < 0 else jnp.where(take_high > 0, WIDE, SPAN)
        low = jnp.int32(max(first, 0) // TILE)
        plan[2 * j] = low
        plan[2 * j + 1] = jnp.maximum((jnp.maximum(jnp.minimum(end_last, limit), 0) + TILE - 1) // TILE, low)
    for i in range(N_TILE):
        pos = i * TILE + lax.broadcasted_iota(jnp.int32, (1, TILE), 1)
        own = jnp.full((1, TILE), -(1 << 20), jnp.int32)
        for start in starts:
            own = jnp.where(pos >= start, start, own)
        start_t[i] = own


def gather_kernel(
    lengths_in, q_in, k_in, v_in, g_in, o_in, norm_in,
    q_out, k_out, v_out, g_out, lse_out, delta_out, start_out, plan_out,
    lengths, grad, output, norm, lse_in, delta_in,
    send_sem, stat_send, recv_sem, z_send, z_recv, z_stat, stat_recv, load_sem, mate_send, mate_recv,
):
    z, x, head, p = place()
    owner, e_own = own_extra(x, head)
    barrier = greet(z, x, head, p)
    loads = [
        pltpu.make_async_copy(src, dst, load_sem.at[n])
        for n, (src, dst) in enumerate(((g_in, grad), (o_in, output), (norm_in, norm), (lengths_in, lengths)))
    ]
    for load in loads:
        load.start()
    helper = shares(x, head) & (head % 2 == 1)
    mate = {"ctx": z * X + x, "head": head // 2 * 2 + 1}
    lower = p < PLANE // 2
    up = {"ctx": ((z + 1) % Z) * X + x, "head": head}
    down = {"ctx": ((z + Z - 1) % Z) * X + x, "head": head}
    pl.semaphore_wait(barrier, PLANE + 1)

    query_side = ((0, q_in, q_out, 0), (3, g_in, g_out, 0))
    key_side = ((1, k_in, k_out, HALO), (2, v_in, v_out, HALO))
    rest = X

    def scatter(side, group, away, extra_away, begin, end):
        def step(i, carry):
            for d in away:
                to_x = (x + d) % X
                peer = to_x * HEAD + (head + turn((i + 2 * d) % HEAD)) % HEAD
                for n, src, dst, base in side:
                    from_, to = src.at[:, columns(peer)], dst.at[0, rows(base, p)]

                    @pl.when(peer == p)
                    def _():
                        pltpu.make_async_copy(from_, to, recv_sem.at[0, group]).start()

                    @pl.when(peer != p)
                    def _():
                        remote(from_, to, send_sem.at[0, n], recv_sem.at[0, group], plane_device(z, peer))

            for d in extra_away:

                @pl.when((i % 2 == 0) & (i < 4))
                def _():
                    e = (x + d) % X * 2 + i // 2
                    extra = extra_owner(e)
                    for n, src, dst, base in side:
                        from_, to = src.at[:, columns(PLANE + e)], dst.at[1, rows(base, p)]

                        @pl.when(extra == p)
                        def _():
                            pltpu.make_async_copy(from_, to, recv_sem.at[1, group]).start()

                        @pl.when(extra != p)
                        def _():
                            remote(from_, to, send_sem.at[1, n], recv_sem.at[1, group], plane_device(z, extra))

            return carry

        lax.fori_loop(begin, end, step, 0)

    def scatter_first(away, extra_away, begin=0, end=HEAD):
        @pl.when(lower)
        def _():
            scatter(query_side, x, away, extra_away, begin, end)

        @pl.when(jnp.logical_not(lower))
        def _():
            scatter(key_side, x, away, extra_away, begin, end)

    def scatter_rest(away, extra_away, begin=0, end=HEAD):
        @pl.when(lower)
        def _():
            scatter(key_side, rest, away, extra_away, begin, end)

        @pl.when(jnp.logical_not(lower))
        def _():
            scatter(query_side, rest, away, extra_away, begin, end)

    block = SPAN // X
    stats = (
        (0, lse_out, pl.ds(0, 2), pl.ds(X, 2)),
        (1, delta_out, pl.ds(0, PLANE // 2), pl.ds(PLANE, PLANE // 2)),
    )

    def forward_stats(slot):
        await_bytes(lse_out.at[slot, pl.ds(0, X)], stat_recv.at[0, slot])
        await_bytes(delta_out.at[slot, pl.ds(0, PLANE)], stat_recv.at[1, slot])
        for n, ref, near, far in stats:
            remote(ref.at[slot, near], ref.at[slot, far], z_stat.at[0, slot, n], z_stat.at[1, slot, n], down)

    def pieces(xs):
        here = pl.ds(pl.multiple_of(HALO + xs * block, block), block)
        there = pl.ds(pl.multiple_of((xs - X // 2) * block, block), block)
        low_here = pl.ds(pl.multiple_of(xs * block, block), block)
        low_there = pl.ds(pl.multiple_of(SPAN + xs * block, block), block)
        return ((k_out, here, there), (v_out, here, there)), ((q_out, low_here, low_there), (g_out, low_here, low_there))

    def hand_over(ref, here, kind):
        remote(ref.at[1, here], ref.at[1, here], mate_send.at[kind], mate_recv.at[kind], mate)

    def forward(slot, xs):
        await_bytes(k_out.at[slot, pl.ds(0, 2 * block)], recv_sem.at[slot, xs])
        keys, queries = pieces(xs)
        if slot == 1:

            @pl.when(xs >= X // 2)
            def _():
                for ref, here, there in keys:
                    hand_over(ref, here, 0)

            @pl.when(xs < X // 2)
            def _():
                for ref, here, there in queries:
                    hand_over(ref, here, 1)

        @pl.when(xs >= X // 2)
        def _():
            for n, (ref, here, there) in enumerate(keys):
                remote(ref.at[slot, here], ref.at[slot, there], z_send.at[slot, xs, n], z_recv.at[slot, xs, n], up)

        @pl.when(xs < X // 2)
        def _():
            for n, (ref, here, there) in enumerate(queries):
                remote(ref.at[slot, here], ref.at[slot, there], z_send.at[slot, xs, n], z_recv.at[slot, xs, n], down)

    sides, ends = (1, 3), (2, 0)

    def finish(slot):
        await_bytes(k_out.at[:, pl.ds(0, 2 * HALO)], recv_sem.at[slot, rest])
        if slot == 1:
            for ref in (k_out, v_out):
                hand_over(ref, pl.ds(HALO, HALO), 0)
            for ref in (q_out, g_out):
                hand_over(ref, pl.ds(HALO, HALO), 1)
        for d in sides + ends:
            xs = (x + X - d) % X
            for n in range(2):
                await_bytes(k_out.at[slot, pl.ds(0, block)], z_recv.at[slot, xs, n])
                await_bytes(k_out.at[slot, pl.ds(0, block)], z_send.at[slot, xs, n])
            if slot == 1:
                keys, queries = pieces(xs)

                @pl.when(xs >= X // 2)
                def _():
                    for ref, here, there in keys:
                        hand_over(ref, there, 0)

                @pl.when(xs < X // 2)
                def _():
                    for ref, here, there in queries:
                        hand_over(ref, there, 1)

        for n, ref, near, far in stats:
            await_bytes(ref.at[slot, near], z_stat.at[0, slot, n])
            await_bytes(ref.at[slot, far], z_stat.at[1, slot, n])
        if slot == 1:
            hand_over(lse_out, pl.ds(0, X + 2), 2)
            hand_over(delta_out, pl.ds(0, PLANE + PLANE // 2), 3)

    def handed_over(sems):
        await_bytes(k_out, sems.at[0])
        await_bytes(q_out, sems.at[1])
        await_bytes(lse_out.at[1], sems.at[2])
        await_bytes(delta_out.at[1], sems.at[3])

    def forward_from(slot, away):
        for d in away:
            forward(slot, (x + X - d) % X)

    scatter_first(sides + ends, sides + ends, 0, 4)
    scatter_first(sides + ends, (), 4, 6)
    for load in loads:
        load.wait()
    local_statistics(p, grad, output, norm, lse_in, delta_in)

    @pl.when(owner)
    def _():
        forward_from(1, sides + ends)

    scatter_first(sides + ends, (), 6, HEAD)
    forward_from(0, sides)
    for j in range(5):
        h = head * 5 + j
        slot = h // PLANE
        target = jnp.where(h < PLANE, h, extra_owner(h - PLANE))
        src, dst = lse_in.at[j], lse_out.at[slot, x]

        @pl.when(target == p)
        def _():
            pltpu.make_async_copy(src, dst, stat_recv.at[0, slot]).start()

        @pl.when(target != p)
        def _():
            remote(src, dst, stat_send.at[j], stat_recv.at[0, slot], plane_device(z, target))

    def delta_main(i, carry):
        peer = (p + i) % PLANE
        remote(delta_in.at[peer], delta_out.at[0, p], stat_send.at[5], stat_recv.at[1, 0], plane_device(z, peer))
        return carry

    lax.fori_loop(1, PLANE, delta_main, 0)
    pltpu.make_async_copy(delta_in.at[p], delta_out.at[0, p], stat_recv.at[1, 0]).start()

    def delta_extra(e, carry):
        peer = extra_owner(e)
        src, dst = delta_in.at[PLANE + e], delta_out.at[1, p]

        @pl.when(peer == p)
        def _():
            pltpu.make_async_copy(src, dst, stat_recv.at[1, 1]).start()

        @pl.when(peer != p)
        def _():
            remote(src, dst, stat_send.at[6], stat_recv.at[1, 1], plane_device(z, peer))

        return carry

    lax.fori_loop(0, EXTRA, delta_extra, 0)

    scatter_rest(sides + ends, sides + ends, 0, HEAD // 2)
    forward_from(0, ends)
    scatter_rest(sides + ends, (), HEAD // 2, HEAD)
    prepare(z, lengths, plan_out, start_out)
    forward_stats(0)

    @pl.when(owner)
    def _():
        forward_stats(1)

    @pl.when(owner)
    def _():
        finish(1)

    finish(0)

    @pl.when(owner)
    def _():
        handed_over(mate_send)

    @pl.when(helper)
    def _():
        handed_over(mate_recv)

    for j in range(5):
        h = head * 5 + j
        target = jnp.where(h < PLANE, h, extra_owner(h - PLANE))

        @pl.when(target != p)
        def _():
            await_bytes(lse_in.at[j], stat_send.at[j])

    await_bytes(delta_in.at[pl.ds(0, PLANE - 1)], stat_send.at[5])
    for n in range(4):
        await_bytes(k_out.at[0, pl.ds(0, (PLANE - 1) * ROWS)], send_sem.at[0, n])

    @pl.when(owner)
    def _():
        await_bytes(delta_in.at[pl.ds(0, EXTRA - 1)], stat_send.at[6])
        for n in range(4):
            await_bytes(k_out.at[0, pl.ds(0, (EXTRA - 1) * ROWS)], send_sem.at[1, n])

    @pl.when(jnp.logical_not(owner))
    def _():
        await_bytes(delta_in.at[pl.ds(0, EXTRA)], stat_send.at[6])
        for n in range(4):
            await_bytes(k_out.at[0, pl.ds(0, EXTRA * ROWS)], send_sem.at[1, n])


def gather(lengths, q, k, v, g, o, norm):
    wide = pltpu.VMEM((2, WIDE, HD), jnp.bfloat16)
    heads = PLANE + EXTRA
    lengths, q, k, v, g, o, norm = (
        pltpu.with_memory_space_constraint(a, pltpu.HBM) for a in (lengths, q, k, v, g, o, norm)
    )
    return pl.pallas_call(
        gather_kernel,
        name="gather_heads",
        out_shape=(
            wide, wide, wide, wide,
            pltpu.VMEM((2, 6, 4, 128), jnp.float32),
            pltpu.VMEM((2, PLANE + PLANE // 2, 1, 128), jnp.float32),
            pltpu.VMEM((N_TILE, 1, TILE), jnp.int32),
            pltpu.SMEM((2 * N_TILE,), jnp.int32),
        ),
        in_specs=[pl.BlockSpec(memory_space=pltpu.HBM)] * 7,
        out_specs=[pl.BlockSpec(memory_space=pltpu.VMEM)] * 7 + [pl.BlockSpec(memory_space=pltpu.SMEM)],
        scratch_shapes=[
            pltpu.SMEM(lengths.shape, lengths.dtype),
            pltpu.VMEM(g.shape, g.dtype),
            pltpu.VMEM(o.shape, o.dtype),
            pltpu.VMEM(norm.shape, norm.dtype),
            pltpu.VMEM((heads // HEAD, 4, 128), jnp.float32),
            pltpu.VMEM((heads, 1, 128), jnp.float32),
            pltpu.SemaphoreType.DMA((2, 4)),
            pltpu.SemaphoreType.DMA((7,)),
            pltpu.SemaphoreType.DMA((2, X + 1)),
            pltpu.SemaphoreType.DMA((2, X, 2)),
            pltpu.SemaphoreType.DMA((2, X, 2)),
            pltpu.SemaphoreType.DMA((2, 2, 2)),
            pltpu.SemaphoreType.DMA((2, 2)),
            pltpu.SemaphoreType.DMA((4,)),
            pltpu.SemaphoreType.DMA((4,)),
            pltpu.SemaphoreType.DMA((4,)),
        ],
        compiler_params=pltpu.CompilerParams(has_side_effects=True, collective_id=0, vmem_limit_bytes=24 * 2**20),
    )(lengths, q, k, v, g, o, norm)


def attention_kernel(
    plan, q_ref, k_ref, v_ref, g_ref, lse_ref, delta_ref, start_t, dq_ref, dk_ref, dv_ref,
    dq_acc, dk_acc, dv_acc, lse_t, delta_t,
):
    scaling = 1.0 / math.sqrt(HD)

    z, x, head, _ = place()
    shared = shares(x, head)
    reach = plan[1]
    for j in range(1, N_TILE):
        reach = jnp.maximum(reach, plan[2 * j + 1])

    def begin_slot(s):
        for i in range(N_TILE):
            lse, delta = [], []
            for c in range(2 * i, 2 * i + 2):
                lse.append(lse_ref[s, c // 4, pl.ds(c % 4, 1), :] * LOG2E)
                delta.append(delta_ref[s, 2 * c] + delta_ref[s, 2 * c + 1])
            lse_t[s, i] = jnp.concatenate(lse, axis=1)
            delta_t[s, i] = jnp.concatenate(delta, axis=1)

        def clear(i, carry):
            dq_acc[s, i] = jnp.zeros((HD, TILE), jnp.float32)
            return carry

        lax.fori_loop(0, reach, clear, 0)

    def end_slot(s):
        def store(i, carry):
            query_rows = pl.ds(pl.multiple_of(i * TILE, TILE), TILE)
            dq_ref[s, query_rows] = (dq_acc[s, i] * scaling).T.astype(jnp.bfloat16)
            return carry

        def store_zero(i, carry):
            query_rows = pl.ds(pl.multiple_of(i * TILE, TILE), TILE)
            dq_ref[s, query_rows] = jnp.zeros((TILE, HD), jnp.bfloat16)
            return carry

        lax.fori_loop(0, reach, store, 0)
        lax.fori_loop(reach, N_TILE, store_zero, 0)

    def key_tile(j, carry):
        key_rows = pl.ds(pl.multiple_of(j * TILE, TILE), TILE)

        begin, end = plan[2 * j], plan[2 * j + 1]

        both = shared & (j % 2 == head % 2)
        alive = end > begin

        def skip(s):
            dk_ref[s, key_rows] = jnp.zeros((TILE, HD), jnp.bfloat16)
            dv_ref[s, key_rows] = jnp.zeros((TILE, HD), jnp.bfloat16)

        def work(slots):
            for s in slots:
                dk_acc[s] = jnp.zeros((TILE, HD), jnp.float32)
                dv_acc[s] = jnp.zeros((TILE, HD), jnp.float32)
            key_pos = j * TILE - HALO + lax.broadcasted_iota(jnp.int32, (TILE, 1), 0)
            keys = [k_ref[s, key_rows] for s in slots]
            values = [v_ref[s, key_rows] for s in slots]
            keys_t = [key.T for key in keys]

            def tiles(i, count):
                query_rows = pl.ds(pl.multiple_of(i * TILE, TILE), TILE * count)

                def along(read):
                    return jnp.concatenate([read(i + m) for m in range(count)], axis=1)

                query_pos = i * TILE + lax.broadcasted_iota(jnp.int32, (1, TILE * count), 1)
                live = (key_pos <= query_pos) & (key_pos >= along(lambda at: start_t[at]))
                raw = [
                    (
                        lax.dot_general(keys[s], q_ref[s, query_rows], NT, preferred_element_type=jnp.float32),
                        lax.dot_general(values[s], g_ref[s, query_rows], NT, preferred_element_type=jnp.float32),
                    )
                    for s in slots
                ]
                low = []
                for s in slots:
                    score, dweight = raw[s]
                    weight = jnp.exp2(score * (scaling * LOG2E) - along(lambda at: lse_t[s, at]))
                    weight = jnp.where(live, weight, 0.0)
                    dscore = weight * (dweight - along(lambda at: delta_t[s, at]))
                    low.append((weight.astype(jnp.bfloat16), dscore.astype(jnp.bfloat16)))
                for s in slots:
                    weight, dscore = low[s]
                    dv_acc[s] += jnp.dot(weight, g_ref[s, query_rows], preferred_element_type=jnp.float32)
                    dk_acc[s] += jnp.dot(dscore, q_ref[s, query_rows], preferred_element_type=jnp.float32)
                    for m in range(count):
                        part = dscore[:, m * TILE : (m + 1) * TILE]
                        dq_acc[s, i + m] += jnp.dot(keys_t[s], part, preferred_element_type=jnp.float32)

            def several(t, carry):
                tiles(begin + AT_ONCE * t, AT_ONCE)
                return carry

            def single(i, carry):
                tiles(i, 1)
                return carry

            groups = (end - begin) // AT_ONCE
            lax.fori_loop(0, groups, several, 0)
            lax.fori_loop(begin + AT_ONCE * groups, end, single, 0)
            for s in slots:
                dk_ref[s, key_rows] = (dk_acc[s] * scaling).astype(jnp.bfloat16)
                dv_ref[s, key_rows] = dv_acc[s].astype(jnp.bfloat16)

        @pl.when(alive & both)
        def _():
            work((0, 1))

        @pl.when(alive & jnp.logical_not(both))
        def _():
            work((0,))

        @pl.when(jnp.logical_not(alive))
        def _():
            skip(0)

        @pl.when(shared & jnp.logical_not(alive & both))
        def _():
            skip(1)

        return carry

    begin_slot(0)

    @pl.when(shared)
    def _():
        begin_slot(1)

    lax.fori_loop(0, N_TILE, key_tile, 0)
    end_slot(0)

    @pl.when(shared)
    def _():
        end_slot(1)


def attention(plan, q, k, v, g, lse, delta, start):
    shape = pltpu.VMEM((2, WIDE, HD), jnp.bfloat16)
    whole = pl.BlockSpec(memory_space=pltpu.VMEM)
    return pl.pallas_call(
        attention_kernel,
        name="attention_backward",
        out_shape=(shape, shape, shape),
        in_specs=[pl.BlockSpec(memory_space=pltpu.SMEM)] + [whole] * 7,
        out_specs=[whole] * 3,
        scratch_shapes=[
            pltpu.VMEM((2, N_TILE, HD, TILE), jnp.float32),
            pltpu.VMEM((2, TILE, HD), jnp.float32),
            pltpu.VMEM((2, TILE, HD), jnp.float32),
            pltpu.VMEM((2, N_TILE, 1, TILE), jnp.float32),
            pltpu.VMEM((2, N_TILE, 1, TILE), jnp.float32),
        ],
        compiler_params=pltpu.CompilerParams(vmem_limit_bytes=24 * 2**20),
    )(plan, q, k, v, g, lse, delta, start)


def scatter_kernel(
    dq_in, dk_in, dv_in, dq_out, dk_out, dv_out,
    halo, part, total, theirs, joined, send_sem, recv_sem, z_send, z_recv, load_sem, mate_send, mate_recv,
):
    z, x, head, p = place()
    owner, e_own = own_extra(x, head)
    up = {"ctx": ((z + 1) % Z) * X + x, "head": head}
    down = {"ctx": ((z + Z - 1) % Z) * X + x, "head": head}
    barrier = greet(z, x, head, p)
    half = PLANE // 2
    ins, outs, bases = (dq_in, dk_in, dv_in), (dq_out, dk_out, dv_out), (0, HALO, HALO)
    sent = (pl.ds(SPAN, HALO), pl.ds(0, HALO), pl.ds(0, HALO))
    kept = (pl.ds(0, HALO), pl.ds(SPAN, HALO), pl.ds(SPAN, HALO))

    helper = shares(x, head) & (head % 2 == 1)
    mate = {"ctx": z * X + x, "head": head // 2 * 2}

    def own(slot, n, at):
        return ins[n].at[0, at] if slot == 0 else joined.at[n, at]

    def join(n):
        await_bytes(theirs.at[n], mate_recv.at[n])

        def step(i, carry):
            at = pl.ds(pl.multiple_of(i * TILE, TILE), TILE)
            joined[n, at] = (ins[n][1, at].astype(jnp.float32) + theirs[n, at].astype(jnp.float32)).astype(jnp.bfloat16)
            return carry

        lax.fori_loop(0, N_TILE, step, 0)

    def exchange(slot):
        for n, device in ((1, down), (0, up), (2, down)):
            remote(own(slot, n, sent[n]), halo.at[slot, n], z_send.at[slot, n], z_recv.at[slot, n], device)
        for n in range(3):
            pltpu.make_async_copy(own(slot, n, kept[n]), part.at[slot, n], load_sem.at[slot, n]).start()

    def deliver(slot, at, n, src, peer):
        dst = outs[n].at[:, columns(at)]

        @pl.when(peer == p)
        def _():
            pltpu.make_async_copy(src, dst, recv_sem.at[n]).start()

        @pl.when(peer != p)
        def _():
            remote(src, dst, send_sem.at[slot, n], recv_sem.at[n], plane_device(z, peer))

    def combine(slot, n):
        await_bytes(part.at[slot, n], load_sem.at[slot, n])
        await_bytes(halo.at[slot, n], z_recv.at[slot, n])
        total[slot, n] = (part[slot, n].astype(jnp.float32) + halo[slot, n].astype(jnp.float32)).astype(jnp.bfloat16)

    def phase(slot, *halves):
        def send(slot, at):
            def step(i, carry):
                to_head = (head + turn(i)) % HEAD
                for c in range(2):
                    for n, upper, combined in halves:
                        near = (x + c) % 2 * HEAD + to_head
                        peer = upper * half + near
                        src = total.at[slot, n, rows(0, near)] if combined else own(slot, n, rows(bases[n], peer))
                        deliver(slot, at, n, src, peer)
                return carry

            lax.fori_loop(0, HEAD, step, 0)

        send(slot, p if slot == 0 else PLANE + e_own)

    def finish(slot):
        for n in range(3):
            await_bytes(halo.at[slot, n], z_send.at[slot, n])
            await_bytes(ins[n].at[slot, pl.ds(0, (PLANE - 1) * ROWS)], send_sem.at[slot, n])

    pl.semaphore_wait(barrier, PLANE + 1)
    @pl.when(helper)
    def _():
        for n in (1, 0, 2):
            remote(ins[n].at[1], theirs.at[n], mate_send.at[n], mate_recv.at[n], mate)

    early = (0, 1, False), (1, 0, False), (2, 0, False)
    exchange(0)
    phase(0, *early)

    @pl.when(owner)
    def _():
        for n in (1, 0, 2):
            join(n)
        exchange(1)
        phase(1, *early)

    def late(slot):
        for n, upper in ((1, 1), (0, 0), (2, 1)):
            combine(slot, n)
            phase(slot, (n, upper, True))

    late(0)

    @pl.when(owner)
    def _():
        late(1)

    @pl.when(helper)
    def _():
        for n in range(3):
            await_bytes(ins[n].at[1], mate_send.at[n])

    for n in range(3):
        await_bytes(outs[n], recv_sem.at[n])
    finish(0)

    @pl.when(owner)
    def _():
        finish(1)


def scatter(dq, dk, dv):
    shape = jax.ShapeDtypeStruct((ROWS, (PLANE + EXTRA) * HD), jnp.bfloat16)
    buffer = pltpu.VMEM((2, 3, HALO, HD), jnp.bfloat16)
    return pl.pallas_call(
        scatter_kernel,
        name="scatter_heads",
        out_shape=(shape, shape, shape),
        in_specs=[pl.BlockSpec(memory_space=pltpu.VMEM)] * 3,
        out_specs=[pl.BlockSpec(memory_space=pl.ANY)] * 3,
        scratch_shapes=[
            buffer, buffer, buffer,
            pltpu.VMEM((3, WIDE, HD), jnp.bfloat16),
            pltpu.VMEM((3, WIDE, HD), jnp.bfloat16),
            pltpu.SemaphoreType.DMA((2, 3)),
            pltpu.SemaphoreType.DMA((3,)),
            pltpu.SemaphoreType.DMA((2, 3)),
            pltpu.SemaphoreType.DMA((2, 3)),
            pltpu.SemaphoreType.DMA((2, 3)),
            pltpu.SemaphoreType.DMA((3,)),
            pltpu.SemaphoreType.DMA((3,)),
        ],
        compiler_params=pltpu.CompilerParams(has_side_effects=True, collective_id=1, vmem_limit_bytes=24 * 2**20),
    )(dq, dk, dv)


def on_device(queries, keys, values, outputs, out_grad, log_norms, doc_lengths):
    q, k, v, g, lse, delta, start, plan = gather(
        doc_lengths, queries, keys, values, out_grad, outputs, log_norms.T
    )
    dq, dk, dv = attention(plan, q, k, v, g, lse, delta, start)
    return scatter(dq, dk, dv)


def solution(mesh):
    row = P(("ctx", "head"), None)
    return jax.shard_map(
        on_device,
        mesh=mesh,
        in_specs=(row, row, row, row, row, P("ctx", "head"), P()),
        out_specs=(row, row, row),
        check_vma=False,
    )
```
